128 devices in a mesh: replica: 8 (over y_lo, z), expert: 16 (over x, y_hi, core).
Axes of the slice: x: 4, y: 4 (y_hi: 2, y_lo: 2; y = y_hi * 2 + y_lo), z: 4, core: 2. Of those that a mesh axis runs over, the one named last changes fastest.
Arguments:
- hidden_states: bfloat16 [8192, 4096], P(('replica', 'expert')), may hold values from -3 to 3
- queries: bfloat16 [8192, 4096], P(('replica', 'expert')), may hold values from -8 to 8
- key_cache: bfloat16 [8192, 256, 256], P(('replica', 'expert')), may hold values from -8 to 8
- value_cache: bfloat16 [8192, 256, 256], P(('replica', 'expert')), may hold values from -6 to 6
- new_keys: bfloat16 [8192, 256], P(('replica', 'expert')), may hold values from -6 to 6
- new_values: bfloat16 [8192, 256], P(('replica', 'expert')), may hold values from -6 to 6
- cache_lengths: int32 [8192], P(('replica', 'expert')), may hold values from 2 to 256
- norm_gain: float32 [4096], replicated, may hold values from 0.1 to 1.9
- expert_ids: int32 [8192, 8], P(('replica', 'expert')), may hold values from 0 to 127, as said below
- route_weights: float32 [8192, 8], P(('replica', 'expert')), may hold values from 0.1 to 1
- finished: int32 [8192], P(('replica', 'expert')), may hold values from 0 to 1
- learner_ids: int32 [8192], P(('replica', 'expert')), may hold values from 0 to 127, as said below
- gate_weight: bfloat16 [16, 4096, 768], P(None, ('replica', 'expert')), may hold values from -0.09375 to 0.09375
- up_weight: bfloat16 [16, 4096, 768], P(None, ('replica', 'expert')), may hold values from -0.09375 to 0.09375
- down_weight: bfloat16 [16, 768, 4096], P(None, None, ('replica', 'expert')), may hold values from -0.21875 to 0.21875
Outputs:
- layer_out: bfloat16 [8192, 4096], P(('replica', 'expert'))
- learner_rows: bfloat16 [16384, 4096], P(('replica', 'expert'))
The draws below stay inside these ranges and needn't reach their ends.
Inputs may be any that keep to these rules, and one draw needn't show every extreme that they name: `expert_ids`: each row names 8 different experts, exactly two of them below 16. In each aligned block of 64 rows no expert below 16 is named by more than 32 rows; in each run of 16 consecutive blocks, starting at block 0, one expert below 16 is named by exactly 32 rows of every block of the run. `learner_ids`: in each aligned block of 64 rows no learner is named by more than 1 row. One learner, the same for every block, is named by exactly 1 row of every block, and those rows are finished.
All inputs are finite; a program needn't handle non-finite values.
Results may differ from the reference program's by a relative error of at most 0.0085.
Values may be sent and summed in bfloat16 or wider, within the bound.
No kernel may reach another device: no remote copies, remote signals or barrier semaphores. Data moves between devices by JAX's collectives and lax.ppermute only.
A program may use at most 128 MiB of HBM per device.

```python
import math
import jax
import jax.numpy as jnp
from jax import lax

D = 4096
HDIM = 128
QHEADS = 32
KVHEADS = 2
HID = 768
ROUTED = 128
TOPK = 8
ROWS_DEV = 64
CTX = 256
EXPERTS = 16
CAP = 32
LEARNERS = 128
SCAP = 1
ROWS = 8192


def learner_plan(key):
    blocks = ROWS // ROWS_DEV
    target = jax.random.randint(jax.random.fold_in(key, 601), (), 0, LEARNERS)
    scores = jax.random.randint(jax.random.fold_in(key, 602), (blocks, LEARNERS), 0, 1 << 20) * LEARNERS + jnp.arange(LEARNERS)
    ranking = jnp.argsort(scores, axis=1, stable=True)
    anchor_pos = jax.random.randint(jax.random.fold_in(key, 603), (blocks,), 0, min(ROWS_DEV, LEARNERS))
    position = jnp.arange(ROWS) % ROWS_DEV
    block_of = jnp.arange(ROWS) // ROWS_DEV
    perm_rows = ranking[block_of]
    own_rank = jnp.take_along_axis(perm_rows, (position % LEARNERS)[:, None], axis=1)[:, 0]
    pinned = jnp.take_along_axis(perm_rows, anchor_pos[block_of][:, None], axis=1)[:, 0]
    destination = (target + own_rank - pinned) % LEARNERS
    return (destination.astype(jnp.int32), target)


def draw_queries(key, part):
    key = jax.random.fold_in(key, 1)
    return jnp.clip(jax.random.normal(key, (ROWS, QHEADS * HDIM), jnp.float32), -6.0, 6.0).astype(jnp.bfloat16)


def draw_key_cache(key, part):
    key = jax.random.fold_in(key, 2)
    return jnp.clip(jax.random.normal(key, (ROWS, CTX, KVHEADS * HDIM), jnp.float32), -6.0, 6.0).astype(jnp.bfloat16)


def draw_expert_ids(key, part):
    key = jax.random.fold_in(key, 3)
    blocks = ROWS // ROWS_DEV
    groups = blocks // EXPERTS
    others = EXPERTS - 1
    hot_expert = jax.random.randint(jax.random.fold_in(key, 1), (groups,), 0, EXPERTS)
    hot_rows = jnp.repeat(hot_expert, EXPERTS * ROWS_DEV)
    scores = jax.random.randint(jax.random.fold_in(key, 2), (blocks, others), 0, 1 << 20) * others + jnp.arange(others)
    ranking = jnp.argsort(scores, axis=1, stable=True)
    shift_by = jax.random.randint(jax.random.fold_in(key, 3), (blocks,), 0, others)
    spread = jax.random.randint(jax.random.fold_in(key, 4), (blocks,), 0, others - 1)
    position = jnp.arange(ROWS) % ROWS_DEV
    block_of = jnp.arange(ROWS) // ROWS_DEV
    perm_rows = ranking[block_of]
    first_off = (position - CAP + shift_by[block_of]) % others
    second_off = (position - CAP + 1 + spread[block_of] + shift_by[block_of]) % others
    first_other = jnp.take_along_axis(perm_rows, first_off[:, None], axis=1)[:, 0]
    second_other = jnp.take_along_axis(perm_rows, second_off[:, None], axis=1)[:, 0]
    first = jnp.where(position < CAP, hot_rows, (hot_rows + 1 + first_other) % EXPERTS)
    second = (hot_rows + 1 + second_other) % EXPERTS
    outside_count = ROUTED - EXPERTS
    outside_scores = jax.random.randint(jax.random.fold_in(key, 5), (ROWS, outside_count), 0, 1 << 20) * outside_count + jnp.arange(outside_count)
    outside = jnp.argsort(outside_scores, axis=1, stable=True)[:, :TOPK - 2] + EXPERTS
    columns = jnp.concatenate([first[:, None], second[:, None], outside], axis=1)
    slot_scores = jax.random.randint(jax.random.fold_in(key, 6), (ROWS, TOPK), 0, 1 << 20) * TOPK + jnp.arange(TOPK)
    slot_order = jnp.argsort(slot_scores, axis=1, stable=True)
    return jnp.take_along_axis(columns, slot_order, axis=1).astype(jnp.int32)


def draw_learner_ids(key, part):
    destination, target = learner_plan(key)
    return destination


def draw_finished(key, part):
    destination, target = learner_plan(key)
    key = jax.random.fold_in(key, 4)
    quarter_draw = jax.random.randint(key, (ROWS,), 0, 4)
    coin_flips = jnp.where(quarter_draw > 0, 1, 0)
    return jnp.where(destination == target, 1, coin_flips).astype(jnp.int32)


def touch_ends(values, key, least, top_value):
    extent = values.shape
    place = [jax.random.randint(jax.random.fold_in(key, axis), (), 0, extent[axis]) for axis in range(len(extent))]
    values = values.at[tuple(place)].set(least)
    longest = extent.index(max(extent))
    place[longest] = (place[longest] + 1) % extent[longest]
    return values.at[tuple(place)].set(top_value)


def block_levels(rng, shape, split, low, top_value):
    loudness = 1.0
    for dim, shards_of in split:
        draws = jax.random.uniform(jax.random.fold_in(jax.random.fold_in(rng, 6), dim), (shards_of,), jnp.float32, low / len(split), top_value / len(split))
        loudness = loudness * jnp.repeat(jnp.exp(draws), shape[dim] // shards_of).reshape((-1,) + (1,) * (len(shape) - 1 - dim))
    return loudness


def bell_draw(stream_key, dims, width, limit, shards=(), kind=jnp.bfloat16):
    entries = width * jax.random.normal(stream_key, dims, jnp.float32)
    if shards:
        entries = entries * block_levels(stream_key, dims, shards, -0.22, 0.18)
    return jnp.clip(entries, -limit, limit).astype(kind)


def setup_inputs(seed: int = 0) -> dict:
    key_list = jax.random.split(jax.random.key(seed), 16)
    return {
        "hidden_states": bell_draw(key_list[0], (ROWS, D), 0.5, 3.0, ((0, 128),)),
        "queries": draw_queries(jax.random.fold_in(key_list[15], 71), 0),
        "key_cache": draw_key_cache(jax.random.fold_in(key_list[15], 71), 0),
        "value_cache": bell_draw(key_list[3], (ROWS, CTX, KVHEADS * HDIM), 1.0, 6.0, ((0, 128),)),
        "new_keys": bell_draw(key_list[4], (ROWS, KVHEADS * HDIM), 1.0, 6.0, ((0, 128),)),
        "new_values": bell_draw(key_list[5], (ROWS, KVHEADS * HDIM), 1.0, 6.0, ((0, 128),)),
        "cache_lengths": touch_ends(jax.random.randint(key_list[6], (ROWS,), 2, CTX + 1), jax.random.fold_in(key_list[6], 1), 2, CTX).astype(jnp.int32),
        "norm_gain": jnp.clip(1.0 + 0.18 * jax.random.normal(key_list[7], (D,), jnp.float32), 0.1, 1.9),
        "expert_ids": draw_expert_ids(jax.random.fold_in(key_list[15], 71), 0),
        "route_weights": jnp.clip(jnp.exp(math.log(1.0) - 2.3025851 * jax.random.uniform(key_list[9], (ROWS, TOPK), jnp.float32) ** block_levels(key_list[9], (ROWS, TOPK), ((0, 128),), -0.2, 0.2)), 0.1, 1.0),
        "finished": draw_finished(jax.random.fold_in(key_list[15], 71), 0),
        "learner_ids": draw_learner_ids(jax.random.fold_in(key_list[15], 71), 0),
        "gate_weight": bell_draw(key_list[12], (EXPERTS, D, HID), D ** -0.5, 0.09375, ((1, 128),)),
        "up_weight": bell_draw(key_list[13], (EXPERTS, D, HID), D ** -0.5, 0.09375, ((1, 128),)),
        "down_weight": bell_draw(key_list[14], (EXPERTS, HID, D), HID ** -0.5, 0.21875, ((2, 128),)),
    }


def attend_block(queries, key_cache, value_cache, new_keys, new_values, cache_lengths):
    row_total = queries.shape[0]
    per_group = QHEADS // KVHEADS
    query_full = queries.astype(jnp.float32).reshape(row_total, KVHEADS, per_group, HDIM)
    keys_full = key_cache.astype(jnp.float32).reshape(row_total, CTX, KVHEADS, HDIM)
    values_full = value_cache.astype(jnp.float32).reshape(row_total, CTX, KVHEADS, HDIM)
    fresh_key = new_keys.astype(jnp.float32).reshape(row_total, KVHEADS, HDIM)
    fresh_value = new_values.astype(jnp.float32).reshape(row_total, KVHEADS, HDIM)
    scaling = 1.0 / math.sqrt(HDIM)
    cached = jnp.einsum('nkgd,nckd->nkgc', query_full, keys_full) * scaling
    usable = jnp.arange(CTX)[None, :] < cache_lengths[:, None]
    cached = jnp.where(usable[:, None, None, :], cached, -jnp.inf)
    own_score = jnp.einsum('nkgd,nkd->nkg', query_full, fresh_key) * scaling
    highest = jnp.maximum(lax.optimization_barrier(jnp.max(cached, axis=-1)), own_score)
    cached_exp = jnp.exp(cached - highest[..., None])
    own_exp = jnp.exp(own_score - highest)
    totals = lax.optimization_barrier(jnp.sum(cached_exp, axis=-1)) + own_exp
    cached_prob = lax.optimization_barrier((cached_exp / totals[..., None]).astype(jnp.bfloat16)).astype(jnp.float32)
    own_prob = lax.optimization_barrier((own_exp / totals).astype(jnp.bfloat16)).astype(jnp.float32)
    mixture = jnp.einsum('nkgc,nckd->nkgd', cached_prob, values_full)
    mixture = mixture + own_prob[..., None] * fresh_value[:, :, None, :]
    return mixture.reshape(row_total, QHEADS * HDIM)

def expert_sum(normed, expert_ids, route_weights, gate_weight, up_weight, down_weight):
    block_size = 512
    inside = expert_ids < EXPERTS
    slot_expert = jnp.where(inside, expert_ids, EXPERTS).reshape(-1).astype(jnp.int32)
    slot_row = (jnp.arange(ROWS * TOPK, dtype=jnp.int32) // TOPK).astype(jnp.int32)
    slot_gate = route_weights.reshape(-1).astype(jnp.float32)
    ordering = jnp.argsort(slot_expert, stable=True).astype(jnp.int32)
    counts = lax.optimization_barrier(jnp.sum((slot_expert[None, :] == jnp.arange(EXPERTS, dtype=jnp.int32)[:, None]).astype(jnp.int32), axis=1)).astype(jnp.int32)
    starts = (jnp.cumsum(counts) - counts).astype(jnp.int32)
    padded_order = jnp.concatenate([ordering, jnp.zeros((block_size,), jnp.int32)])

    def per_expert(expert, running):
        expert_gate = gate_weight[expert]
        expert_up = up_weight[expert]
        expert_down = down_weight[expert]
        block_total = ((counts[expert] + block_size - 1) // block_size).astype(jnp.int32)

        def per_block(block_index, inner):
            first_slot = (starts[expert] + block_index * block_size).astype(jnp.int32)
            slot_ids = lax.dynamic_slice(padded_order, (first_slot,), (block_size,))
            slot_live = block_index * block_size + jnp.arange(block_size, dtype=jnp.int32) < counts[expert]
            slot_rows = slot_row[slot_ids]
            inputs = normed[slot_rows]
            gate_part = jnp.dot(inputs, expert_gate, preferred_element_type=jnp.float32)
            up_part = jnp.dot(inputs, expert_up, preferred_element_type=jnp.float32)
            activated = (jax.nn.silu(gate_part) * up_part).astype(jnp.bfloat16)
            expert_out = jnp.dot(activated, expert_down, preferred_element_type=jnp.float32).astype(jnp.bfloat16)
            expert_out = lax.optimization_barrier(expert_out).astype(jnp.float32)
            slot_weight = jnp.where(slot_live, slot_gate[slot_ids], 0.0)
            return inner.at[slot_rows].add(slot_weight[:, None] * expert_out)
        return lax.fori_loop(jnp.int32(0), block_total, per_block, running)
    running = jnp.zeros((ROWS, D), jnp.float32)
    return lax.fori_loop(0, EXPERTS, per_expert, running)

def deliver(layer_out, finished, learner_ids):
    destination = learner_ids.reshape(LEARNERS, ROWS_DEV)
    finished_rows = finished.reshape(LEARNERS, ROWS_DEV) > 0
    earlier = jnp.arange(ROWS_DEV)[None, :] < jnp.arange(ROWS_DEV)[:, None]
    same_target = (destination[:, :, None] == destination[:, None, :]) & finished_rows[:, None, :] & earlier[None]
    slot_rank = lax.optimization_barrier(jnp.sum(same_target.astype(jnp.int32), axis=2)).astype(jnp.int32)
    source = jnp.arange(LEARNERS, dtype=jnp.int32)[:, None]
    target = destination * (LEARNERS * SCAP) + source * SCAP + slot_rank
    total_slots = LEARNERS * LEARNERS * SCAP
    target = jnp.where(finished_rows, target, total_slots).reshape(-1).astype(jnp.int32)
    return jnp.zeros((total_slots, D), jnp.bfloat16).at[target].set(layer_out, mode='drop')

def reference(hidden_states, queries, key_cache, value_cache, new_keys, new_values, cache_lengths, norm_gain, expert_ids, route_weights, finished, learner_ids, gate_weight, up_weight, down_weight):
    block_rows = math.gcd(512, ROWS)
    block_count = ROWS // block_rows

    def blockwise(array):
        return array.reshape((block_count, block_rows) + array.shape[1:])
    attended = lax.map(lambda pieces: attend_block(*pieces), (blockwise(queries), blockwise(key_cache), blockwise(value_cache), blockwise(new_keys), blockwise(new_values), blockwise(cache_lengths)))
    attended = attended.reshape(ROWS, D)
    middle = hidden_states.astype(jnp.float32) + attended
    spread = lax.optimization_barrier(jnp.mean(middle * middle, axis=-1, keepdims=True))
    normed = (middle * lax.rsqrt(spread + 1e-06) * norm_gain.astype(jnp.float32)).astype(jnp.bfloat16)
    routed = expert_sum(normed, expert_ids, route_weights, gate_weight, up_weight, down_weight)
    layer_out = (middle + routed).astype(jnp.bfloat16)
    learner_rows = deliver(layer_out, finished, learner_ids)
    return (layer_out, learner_rows)
```

```python
import math

import jax
import jax.numpy as jnp
from jax import lax
from jax.experimental import pallas as pl
from jax.experimental.pallas import tpu as pltpu
from jax.sharding import Mesh
from jax.sharding import PartitionSpec as P

HDIM = 128
QHEADS = 32
KVHEADS = 2

AXES = ("ylo", "z", "x", "yhi", "core")
PLANE = ("ylo", "x", "yhi")
RING = 4
ZUP = [(i, (i + 1) % RING) for i in range(RING)]
ZDOWN = [(i, (i - 1) % RING) for i in range(RING)]
SWAP = [(0, 1), (1, 0)]


def attend_rows(queries, key_cache, value_cache, new_keys, new_values, cache_lengths):
    row_total = queries.shape[0]
    context = key_cache.shape[1]
    per_group = QHEADS // KVHEADS
    query_parts = queries.reshape(row_total, KVHEADS, per_group, HDIM)
    key_parts = key_cache.reshape(row_total, context, KVHEADS, HDIM)
    value_parts = value_cache.reshape(row_total, context, KVHEADS, HDIM)
    fresh_key = new_keys.reshape(row_total, KVHEADS, HDIM)
    fresh_value = new_values.astype(jnp.float32).reshape(row_total, KVHEADS, HDIM)
    scaling = 1.0 / math.sqrt(HDIM)
    cached = (
        jnp.einsum("nkgd,nckd->nkgc", query_parts, key_parts, preferred_element_type=jnp.float32)
        * scaling
    )
    usable = jnp.arange(context)[None, :] < cache_lengths[:, None]
    cached = jnp.where(usable[:, None, None, :], cached, -jnp.inf)
    own_score = (
        jnp.einsum("nkgd,nkd->nkg", query_parts, fresh_key, preferred_element_type=jnp.float32)
        * scaling
    )
    highest = jnp.maximum(jnp.max(cached, axis=-1), own_score)
    cached_exp = jnp.exp(cached - highest[..., None])
    own_exp = jnp.exp(own_score - highest)
    totals = jnp.sum(cached_exp, axis=-1) + own_exp
    cached_prob = (cached_exp / totals[..., None]).astype(jnp.bfloat16)
    own_prob = (own_exp / totals).astype(jnp.bfloat16).astype(jnp.float32)
    mixture = jnp.einsum(
        "nkgc,nckd->nkgd", cached_prob, value_parts, preferred_element_type=jnp.float32
    )
    mixture = mixture + own_prob[..., None] * fresh_value[:, :, None, :]
    return mixture.reshape(row_total, QHEADS * HDIM)


def spread_piece(piece):
    half = piece.shape[0] // 2
    prev = lax.ppermute(piece, "z", ZUP)
    succ = lax.ppermute(piece, "z", ZDOWN)
    far_a = lax.ppermute(prev[:half], "z", ZUP)
    far_b = lax.ppermute(succ[half:], "z", ZDOWN)
    mine = [piece, prev, succ, far_a, far_b]
    other = [lax.ppermute(part, "core", SWAP) for part in mine]
    return mine + other


def place_copies(place_ref, parts, kinds, scratch, sem, ylos):
    z = place_ref[0]
    core = place_ref[1]
    copies = []
    for index, part in enumerate(parts):
        which = index % 5
        c = core if index < 5 else 1 - core
        step = (0, RING - 1, 1, 2, 2)[which]
        zz = lax.rem(z + step, RING)
        halves = part.shape[0]
        for lo in range(halves):
            low = lo if which != 4 else lo + ylos - halves
            if kinds:
                for kind in range(kinds):
                    copies.append(
                        pltpu.make_async_copy(
                            part.at[lo, :, kind], scratch.at[kind, low, zz, :, c], sem
                        )
                    )
            else:
                copies.append(
                    pltpu.make_async_copy(part.at[lo], scratch.at[low, zz, :, c], sem)
                )
    return copies


def hidden_kernel(place_ref, rows_ref, *refs):
    parts = refs[:10]
    out_ref, scratch, sem = refs[10:]
    copies = place_copies(place_ref, parts, 2, scratch, sem, 2)
    for copy in copies:
        copy.start()
    for copy in copies:
        copy.wait()
    width = out_ref.shape[1]
    step = 256

    @pl.loop(0, width // step)
    def _(i):
        cols = pl.ds(pl.multiple_of(i * step, step), step)
        rows = rows_ref[...]
        depth = rows.shape[1]
        gate = scratch[0, :, :, :, :, :, cols].reshape(depth, step)
        up = scratch[1, :, :, :, :, :, cols].reshape(depth, step)
        g = jnp.dot(rows, gate, preferred_element_type=jnp.float32)
        u = jnp.dot(rows, up, preferred_element_type=jnp.float32)
        out_ref[:, cols] = (g / (1.0 + jnp.exp(-g)) * u).astype(out_ref.dtype)


def hidden_call(place, rows, parts):
    count, depth = rows.shape
    width = parts[0].shape[-1]
    vmem = pl.BlockSpec(memory_space=pltpu.VMEM)
    return pl.pallas_call(
        hidden_kernel,
        out_shape=jax.ShapeDtypeStruct((count, width), jnp.bfloat16),
        in_specs=[pl.BlockSpec(memory_space=pltpu.SMEM), vmem]
        + [pl.BlockSpec(memory_space=pl.ANY)] * 10,
        out_specs=vmem,
        scratch_shapes=[
            pltpu.VMEM((2, 2, RING, 8, 2, 32, width), jnp.bfloat16),
            pltpu.SemaphoreType.DMA,
        ],
        compiler_params=pltpu.CompilerParams(vmem_limit_bytes=40 * 1024 * 1024),
        cost_estimate=pl.CostEstimate(
            flops=4 * count * depth * width,
            bytes_accessed=4 * depth * width + 2 * count * depth,
            transcendentals=count * width,
        ),
    )(place, rows, *parts)


def project_kernel(place_ref, hidden_ref, *refs):
    parts = refs[:10]
    out_ref, scratch, sem = refs[10:]
    ylos = scratch.shape[0]
    copies = place_copies(place_ref, parts, 0, scratch, sem, ylos)
    for copy in copies:
        copy.start()
    for copy in copies:
        copy.wait()
    hidden = hidden_ref[...]
    for lo in range(ylos):
        for zz in range(RING):
            weight = scratch[lo, zz].reshape(512, hidden.shape[1])
            out_ref[:, lo * 2048 + zz * 512 : lo * 2048 + (zz + 1) * 512] = lax.dot_general(
                hidden, weight, (((1,), (1,)), ((), ())), preferred_element_type=jnp.float32
            ).astype(out_ref.dtype)


def project_call(place, hidden, parts, ylos):
    count, width = hidden.shape
    depth = ylos * 2048
    vmem = pl.BlockSpec(memory_space=pltpu.VMEM)
    return pl.pallas_call(
        project_kernel,
        out_shape=jax.ShapeDtypeStruct((count, depth), jnp.bfloat16),
        in_specs=[pl.BlockSpec(memory_space=pltpu.SMEM), vmem]
        + [pl.BlockSpec(memory_space=pl.ANY)] * 10,
        out_specs=vmem,
        scratch_shapes=[
            pltpu.VMEM((ylos, RING, 8, 2, 32, width), jnp.bfloat16),
            pltpu.SemaphoreType.DMA,
        ],
        compiler_params=pltpu.CompilerParams(vmem_limit_bytes=40 * 1024 * 1024),
        cost_estimate=pl.CostEstimate(
            flops=2 * count * depth * width,
            bytes_accessed=2 * depth * width + 2 * count * depth,
            transcendentals=0,
        ),
    )(place, hidden, *parts)


def shards(
    hidden_states,
    queries,
    key_cache,
    value_cache,
    new_keys,
    new_values,
    cache_lengths,
    norm_gain,
    expert_ids,
    route_weights,
    finished,
    learner_ids,
    gate_weight,
    up_weight,
    down_weight,
):
    experts = 16
    learners = 128
    row_count, model_width = hidden_states.shape
    capacity = row_count // 2
    slots = experts * capacity
    place = jnp.stack([lax.axis_index("z"), lax.axis_index("core")]).astype(jnp.int32)

    pair = jnp.stack([gate_weight, up_weight], axis=1)
    pair = lax.all_to_all(pair, PLANE, split_axis=0, concat_axis=0, tiled=True)
    down = jnp.swapaxes(down_weight, 1, 2)
    down = lax.all_to_all(down, PLANE, split_axis=0, concat_axis=0, tiled=True)
    width = down.shape[-1]
    pair_parts = [
        part.reshape(-1, 8, 2, 32, width)
        for part in spread_piece(pair.reshape(16, 2, 32, width))
    ]
    down_parts = [
        part.reshape(-1, 8, 32, width) for part in spread_piece(down.reshape(16, 32, width))
    ]

    attended = attend_rows(queries, key_cache, value_cache, new_keys, new_values, cache_lengths)
    middle = hidden_states.astype(jnp.float32) + attended
    spread = jnp.mean(middle * middle, axis=-1, keepdims=True)
    normed = (middle * lax.rsqrt(spread + 1e-06) * norm_gain).astype(jnp.bfloat16)

    expert_range = jnp.arange(experts, dtype=jnp.int32)
    hit_table = expert_ids[:, :, None] == expert_range[None, None, :]
    matched = jnp.any(hit_table, axis=1)
    slot_gate = jnp.sum(jnp.where(hit_table, route_weights[:, :, None], 0.0), axis=1)
    row_range = jnp.arange(row_count, dtype=jnp.int32)
    earlier = row_range[None, :] < row_range[:, None]
    slot_rank = jnp.sum(
        jnp.where(earlier[:, :, None] & matched[None, :, :], 1, 0).astype(jnp.int32), axis=1
    )
    slot_range = jnp.arange(capacity, dtype=jnp.int32)
    chosen = matched[:, :, None] & (slot_rank[:, :, None] == slot_range[None, None, :])
    pick = chosen.reshape(row_count, slots).astype(jnp.bfloat16)
    weigh = jnp.where(chosen, slot_gate[:, :, None], 0.0).reshape(row_count, slots)
    weigh_high = weigh.astype(jnp.bfloat16)
    weigh_low = (weigh - weigh_high.astype(jnp.float32)).astype(jnp.bfloat16)

    outgoing = lax.dot_general(
        pick, normed, (((0,), (0,)), ((), ())), preferred_element_type=jnp.float32
    ).astype(jnp.bfloat16)
    received = lax.all_to_all(
        outgoing.reshape(experts, capacity, model_width),
        PLANE,
        split_axis=0,
        concat_axis=0,
        tiled=True,
    ).reshape(slots, model_width)

    hidden = hidden_call(place, received, pair_parts)
    expert_out = project_call(place, hidden, down_parts, 2)
    returned = lax.all_to_all(
        expert_out.reshape(experts, capacity, model_width),
        PLANE,
        split_axis=0,
        concat_axis=0,
        tiled=True,
    ).reshape(slots, model_width)
    routed = jnp.dot(weigh_high, returned, preferred_element_type=jnp.float32) + jnp.dot(
        weigh_low, returned, preferred_element_type=jnp.float32
    )
    layer_out = (middle + routed).astype(jnp.bfloat16)

    per_pair = 1
    finished_rows = finished > 0
    same_target = (learner_ids[:, None] == learner_ids[None, :]) & finished_rows[None, :] & earlier
    learner_rank = jnp.sum(same_target.astype(jnp.int32), axis=1)
    slot_of_row = learner_ids * per_pair + learner_rank
    slot_span = jnp.arange(learners * per_pair, dtype=jnp.int32)
    picked = finished_rows[None, :] & (slot_of_row[None, :] == slot_span[:, None])
    parcel = jnp.dot(
        picked.astype(jnp.bfloat16), layer_out, preferred_element_type=jnp.float32
    ).astype(jnp.bfloat16)
    parcel = parcel.reshape(learners, per_pair, model_width)
    arrived = lax.all_to_all(parcel, AXES, split_axis=0, concat_axis=0, tiled=True)
    return (layer_out, arrived.reshape(-1, model_width))


def solution(mesh):
    fine = Mesh(mesh.devices.reshape(2, 4, 4, 2, 2), AXES)
    rows = P(AXES)
    placed = (
        P(AXES, None),
        P(AXES, None),
        P(AXES, None, None),
        P(AXES, None, None),
        P(AXES, None),
        P(AXES, None),
        P(AXES),
        P(),
        P(AXES, None),
        P(AXES, None),
        P(AXES),
        P(AXES),
        P(None, AXES, None),
        P(None, AXES, None),
        P(None, None, AXES),
    )
    return jax.shard_map(
        shards,
        mesh=fine,
        in_specs=placed,
        out_specs=(P(AXES, None), P(AXES, None)),
        check_vma=False,
    )
```

```python
import functools
import math

import jax
import jax.numpy as jnp
from jax import lax
from jax.experimental import pallas as pl
from jax.experimental.pallas import tpu as pltpu
from jax.sharding import Mesh
from jax.sharding import PartitionSpec as P

HDIM = 128
QHEADS = 32
KVHEADS = 2

AXES = ("ylo", "z", "x", "yhi", "core")
PLANE = ("ylo", "x", "yhi")
RING = 4
ZUP = [(i, (i + 1) % RING) for i in range(RING)]
ZDOWN = [(i, (i - 1) % RING) for i in range(RING)]
SWAP = [(0, 1), (1, 0)]
LINE = 128
LINES = 32
MIB = 1024 * 1024


def attend_rows(queries, key_cache, value_cache, new_keys, new_values, cache_lengths):
    row_total = queries.shape[0]
    context = key_cache.shape[1]
    per_group = QHEADS // KVHEADS
    query_parts = queries.reshape(row_total, KVHEADS, per_group, HDIM)
    key_parts = key_cache.reshape(row_total, context, KVHEADS, HDIM)
    value_parts = value_cache.reshape(row_total, context, KVHEADS, HDIM)
    fresh_key = new_keys.reshape(row_total, KVHEADS, HDIM)
    fresh_value = new_values.astype(jnp.float32).reshape(row_total, KVHEADS, HDIM)
    scaling = 1.0 / math.sqrt(HDIM)
    cached = (
        jnp.einsum("nkgd,nckd->nkgc", query_parts, key_parts, preferred_element_type=jnp.float32)
        * scaling
    )
    usable = jnp.arange(context)[None, :] < cache_lengths[:, None]
    cached = jnp.where(usable[:, None, None, :], cached, -jnp.inf)
    own_score = (
        jnp.einsum("nkgd,nkd->nkg", query_parts, fresh_key, preferred_element_type=jnp.float32)
        * scaling
    )
    highest = jnp.maximum(jnp.max(cached, axis=-1), own_score)
    cached_exp = jnp.exp(cached - highest[..., None])
    own_exp = jnp.exp(own_score - highest)
    totals = jnp.sum(cached_exp, axis=-1) + own_exp
    cached_prob = (cached_exp / totals[..., None]).astype(jnp.bfloat16)
    own_prob = (own_exp / totals).astype(jnp.bfloat16).astype(jnp.float32)
    mixture = jnp.einsum(
        "nkgc,nckd->nkgd", cached_prob, value_parts, preferred_element_type=jnp.float32
    )
    mixture = mixture + own_prob[..., None] * fresh_value[:, :, None, :]
    return mixture.reshape(row_total, QHEADS * HDIM)


def spread_piece(piece, way):
    half = piece.shape[0] // 2
    prev = lax.ppermute(piece, "z", ZUP)
    succ = lax.ppermute(piece, "z", ZDOWN)
    if way > 0:
        far = [lax.ppermute(prev, "z", ZUP)]
    elif way < 0:
        far = [lax.ppermute(succ, "z", ZDOWN)]
    else:
        far = [
            lax.ppermute(prev[:half], "z", ZUP),
            lax.ppermute(succ[half:], "z", ZDOWN),
        ]
    mine = [piece, prev, succ] + far
    other = [lax.ppermute(part, "core", SWAP) for part in mine]
    return [part.reshape(-1, 8, 32, part.shape[-1]) for part in mine + other]


def place_copies(place_ref, parts, scratch, sem):
    z = place_ref[0]
    core = place_ref[1]
    count = len(parts) // 2
    copies = []
    for index, part in enumerate(parts):
        which = index % count
        c = core if index < count else 1 - core
        zz = lax.rem(z + (0, RING - 1, 1, 2, 2)[which], RING)
        for lo in range(part.shape[0]):
            low = lo if which != 4 else 1
            copies.append(pltpu.make_async_copy(part.at[lo], scratch.at[low, zz, :, c], sem))
    return copies


def hidden_kernel(gate_count, place_ref, rows_any, *refs):
    gate_parts = refs[:gate_count]
    up_parts = refs[gate_count:-6]
    out_ref, rows_ref, gate_ref, up_ref, acc_ref, sem = refs[-6:]
    rows_copy = pltpu.make_async_copy(rows_any, rows_ref, sem.at[2])
    rows_copy.start()
    gate_copies = place_copies(place_ref, gate_parts, gate_ref, sem.at[0])
    up_copies = place_copies(place_ref, up_parts, up_ref, sem.at[1])
    for copy in gate_copies + up_copies:
        copy.start()
    rows_copy.wait()
    for copy in gate_copies:
        copy.wait()
    depth = rows_ref.shape[1]
    width = out_ref.shape[1]
    step = 256

    @pl.loop(0, width // step)
    def _(i):
        cols = pl.ds(pl.multiple_of(i * step, step), step)
        gate = gate_ref[:, :, :, :, :, cols].reshape(depth, step)
        g = jnp.dot(rows_ref[...], gate, preferred_element_type=jnp.float32)
        acc_ref[:, cols] = g / (1.0 + jnp.exp(-g))

    for copy in up_copies:
        copy.wait()

    @pl.loop(0, width // step)
    def _(i):
        cols = pl.ds(pl.multiple_of(i * step, step), step)
        up = up_ref[:, :, :, :, :, cols].reshape(depth, step)
        u = jnp.dot(rows_ref[...], up, preferred_element_type=jnp.float32)
        out_ref[:, cols] = (acc_ref[:, cols] * u).astype(out_ref.dtype)


def hidden_call(place, rows, gate_parts, up_parts):
    count, depth = rows.shape
    width = gate_parts[0].shape[-1]
    hbm = pl.BlockSpec(memory_space=pl.ANY)
    weight = pltpu.VMEM((2, RING, 8, 2, 32, width), jnp.bfloat16)
    return pl.pallas_call(
        functools.partial(hidden_kernel, len(gate_parts)),
        out_shape=jax.ShapeDtypeStruct((count, width), jnp.bfloat16),
        in_specs=[pl.BlockSpec(memory_space=pltpu.SMEM)]
        + [hbm] * (1 + len(gate_parts) + len(up_parts)),
        out_specs=pl.BlockSpec(memory_space=pltpu.VMEM),
        scratch_shapes=[
            pltpu.VMEM((count, depth), jnp.bfloat16),
            weight,
            weight,
            pltpu.VMEM((count, width), jnp.float32),
            pltpu.SemaphoreType.DMA((3,)),
        ],
        compiler_params=pltpu.CompilerParams(vmem_limit_bytes=24 * MIB),
        cost_estimate=pl.CostEstimate(
            flops=4 * count * depth * width,
            bytes_accessed=4 * depth * width + 2 * count * depth,
            transcendentals=count * width,
        ),
        name="hidden",
    )(place, rows, *gate_parts, *up_parts)


def project_kernel(place_ref, hidden_ref, *refs):
    parts = refs[:-5]
    out_any, scratch, out_ref, sem, out_sem = refs[-5:]
    copies = place_copies(place_ref, parts, scratch, sem)
    for copy in copies:
        copy.start()
    for copy in copies:
        copy.wait()
    hidden = hidden_ref[...]
    outs = []
    for chunk in range(2 * RING):
        weight = scratch[chunk // RING, chunk % RING].reshape(512, hidden.shape[1])
        cols = slice(chunk * 512, (chunk + 1) * 512)
        out_ref[:, cols] = lax.dot_general(
            hidden, weight, (((1,), (1,)), ((), ())), preferred_element_type=jnp.float32
        ).astype(out_ref.dtype)
        out = pltpu.make_async_copy(out_ref.at[:, cols], out_any.at[:, cols], out_sem.at[chunk])
        out.start()
        outs.append(out)
    for out in outs:
        out.wait()


def project_call(place, hidden, parts):
    count, width = hidden.shape
    depth = 4096
    hbm = pl.BlockSpec(memory_space=pl.ANY)
    return pl.pallas_call(
        project_kernel,
        out_shape=jax.ShapeDtypeStruct((count, depth), jnp.bfloat16),
        in_specs=[
            pl.BlockSpec(memory_space=pltpu.SMEM),
            pl.BlockSpec(memory_space=pltpu.VMEM),
        ]
        + [hbm] * len(parts),
        out_specs=hbm,
        scratch_shapes=[
            pltpu.VMEM((2, RING, 8, 2, 32, width), jnp.bfloat16),
            pltpu.VMEM((count, depth), jnp.bfloat16),
            pltpu.SemaphoreType.DMA,
            pltpu.SemaphoreType.DMA((2 * RING,)),
        ],
        compiler_params=pltpu.CompilerParams(vmem_limit_bytes=18 * MIB),
        cost_estimate=pl.CostEstimate(
            flops=2 * count * depth * width,
            bytes_accessed=2 * depth * width + 2 * count * depth,
            transcendentals=0,
        ),
        name="project",
    )(place, hidden, *parts)


def combine_kernel(high_ref, low_ref, picked_ref, middle_ref, back_ref, layer_ref, parcel_ref, rows_ref):
    step = pl.program_id(0)
    back = back_ref[...]
    routed = jnp.dot(high_ref[...], back, preferred_element_type=jnp.float32) + jnp.dot(
        low_ref[...], back, preferred_element_type=jnp.float32
    )
    layer = (middle_ref[...] + routed).astype(jnp.bfloat16)
    layer_ref[...] = layer
    lines = picked_ref.shape[0]
    taken = jnp.dot(picked_ref[...], layer, preferred_element_type=jnp.float32)
    per_step = layer.shape[1] // LINE
    for part in range(per_step):
        rows_ref[pl.ds(step * per_step + part, lines, stride=LINES), :] = taken[
            :, part * LINE : (part + 1) * LINE
        ]

    @pl.when(step == pl.num_programs(0) - 1)
    def _():
        parcel_ref[...] = rows_ref[...].reshape(parcel_ref.shape).astype(parcel_ref.dtype)


def combine_call(high, low, picked, middle, back):
    rows, width = middle.shape
    slots = back.shape[0]
    learners = picked.shape[0]
    step = 512
    whole = lambda shape: pl.BlockSpec(shape, lambda i: (0,) * len(shape))
    column = lambda count: pl.BlockSpec((count, step), lambda i: (0, i))
    return pl.pallas_call(
        combine_kernel,
        grid=(width // step,),
        out_shape=(
            jax.ShapeDtypeStruct((rows, width), jnp.bfloat16),
            jax.ShapeDtypeStruct((learners, LINES, LINE), jnp.bfloat16),
        ),
        in_specs=[
            whole((rows, slots)),
            whole((rows, slots)),
            whole((learners, rows)),
            column(rows),
            column(slots),
        ],
        out_specs=(column(rows), whole((learners, LINES, LINE))),
        scratch_shapes=[pltpu.VMEM((learners * LINES, LINE), jnp.float32)],
        compiler_params=pltpu.CompilerParams(vmem_limit_bytes=16 * MIB),
        name="combine",
    )(high, low, picked, middle, back)


def unpack_kernel(lines_ref, out_ref, rows_ref):
    count = lines_ref.shape[0]
    rows_ref[...] = lines_ref[...].reshape(rows_ref.shape).astype(jnp.float32)
    for part in range(LINES):
        out_ref[:, part * LINE : (part + 1) * LINE] = rows_ref[
            pl.ds(part, count, stride=LINES), :
        ].astype(out_ref.dtype)


def unpack_call(lines):
    count = lines.shape[0]
    vmem = pl.BlockSpec(memory_space=pltpu.VMEM)
    return pl.pallas_call(
        unpack_kernel,
        out_shape=jax.ShapeDtypeStruct((count, LINES * LINE), jnp.bfloat16),
        in_specs=[vmem],
        out_specs=vmem,
        scratch_shapes=[pltpu.VMEM((count * LINES, LINE), jnp.float32)],
        compiler_params=pltpu.CompilerParams(vmem_limit_bytes=16 * MIB),
        name="unpack",
    )(lines)


def shards(
    hidden_states,
    queries,
    key_cache,
    value_cache,
    new_keys,
    new_values,
    cache_lengths,
    norm_gain,
    expert_ids,
    route_weights,
    finished,
    learner_ids,
    gate_weight,
    up_weight,
    down_weight,
):
    experts = 16
    learners = 128
    row_count, model_width = hidden_states.shape
    capacity = row_count // 2
    slots = experts * capacity
    place = jnp.stack([lax.axis_index("z"), lax.axis_index("core")]).astype(jnp.int32)

    to_chip = lambda part: lax.all_to_all(part, PLANE, split_axis=0, concat_axis=0, tiled=True)
    gate = to_chip(gate_weight)
    up = to_chip(up_weight)
    down = to_chip(jnp.swapaxes(down_weight, 1, 2))
    gate_parts = spread_piece(gate, 1)
    up_parts = spread_piece(up, -1)
    down_parts = spread_piece(down, 0)

    queries, _ = lax.optimization_barrier((queries, gate))
    attended = attend_rows(queries, key_cache, value_cache, new_keys, new_values, cache_lengths)
    middle = hidden_states.astype(jnp.float32) + attended
    spread = jnp.mean(middle * middle, axis=-1, keepdims=True)
    normed = (middle * lax.rsqrt(spread + 1e-06) * norm_gain).astype(jnp.bfloat16)

    expert_range = jnp.arange(experts, dtype=jnp.int32)
    hit_table = expert_ids[:, :, None] == expert_range[None, None, :]
    matched = jnp.any(hit_table, axis=1)
    slot_gate = jnp.sum(jnp.where(hit_table, route_weights[:, :, None], 0.0), axis=1)
    row_range = jnp.arange(row_count, dtype=jnp.int32)
    earlier = row_range[None, :] < row_range[:, None]
    slot_rank = jnp.sum(
        jnp.where(earlier[:, :, None] & matched[None, :, :], 1, 0).astype(jnp.int32), axis=1
    )
    slot_range = jnp.arange(capacity, dtype=jnp.int32)
    chosen = matched[:, :, None] & (slot_rank[:, :, None] == slot_range[None, None, :])
    pick = chosen.reshape(row_count, slots).astype(jnp.bfloat16)
    weigh = jnp.where(chosen, slot_gate[:, :, None], 0.0).reshape(row_count, slots)
    weigh_high = weigh.astype(jnp.bfloat16)
    weigh_low = (weigh - weigh_high.astype(jnp.float32)).astype(jnp.bfloat16)

    outgoing = lax.dot_general(
        pick, normed, (((0,), (0,)), ((), ())), preferred_element_type=jnp.float32
    ).astype(jnp.bfloat16)
    outgoing, _, _, _ = lax.optimization_barrier((outgoing, gate_parts[1], gate_parts[2], down))
    received = lax.all_to_all(
        outgoing.reshape(experts, capacity, model_width),
        PLANE,
        split_axis=0,
        concat_axis=0,
        tiled=True,
    ).reshape(slots, model_width)

    hidden = hidden_call(place, received, gate_parts, up_parts)
    expert_out = project_call(place, hidden, down_parts)
    returned = lax.all_to_all(
        expert_out.reshape(experts, capacity, model_width),
        PLANE,
        split_axis=0,
        concat_axis=0,
        tiled=True,
    ).reshape(slots, model_width)

    finished_rows = finished > 0
    same_target = (learner_ids[:, None] == learner_ids[None, :]) & finished_rows[None, :] & earlier
    learner_rank = jnp.sum(same_target.astype(jnp.int32), axis=1)
    slot_of_row = learner_ids + learner_rank
    slot_span = jnp.arange(learners, dtype=jnp.int32)
    picked = finished_rows[None, :] & (slot_of_row[None, :] == slot_span[:, None])
    layer_out, parcel = combine_call(
        weigh_high, weigh_low, picked.astype(jnp.bfloat16), middle, returned
    )
    arrived = lax.all_to_all(parcel, AXES, split_axis=0, concat_axis=0, tiled=True)
    return (layer_out, unpack_call(arrived))


def solution(mesh):
    fine = Mesh(mesh.devices.reshape(2, 4, 4, 2, 2), AXES)
    rows = P(AXES)
    placed = (
        P(AXES, None),
        P(AXES, None),
        P(AXES, None, None),
        P(AXES, None, None),
        P(AXES, None),
        P(AXES, None),
        P(AXES),
        P(),
        P(AXES, None),
        P(AXES, None),
        P(AXES),
        P(AXES),
        P(None, AXES, None),
        P(None, AXES, None),
        P(None, None, AXES),
    )
    return jax.shard_map(
        shards,
        mesh=fine,
        in_specs=placed,
        out_specs=(P(AXES, None), P(AXES, None)),
        check_vma=False,
    )
```

```python
import math

import jax
import jax.numpy as jnp
from jax import lax
from jax.experimental import pallas as pl
from jax.experimental.pallas import tpu as pltpu
from jax.sharding import Mesh
from jax.sharding import PartitionSpec as P

HDIM = 128
QHEADS = 32
KVHEADS = 2

AXES = ("ylo", "z", "x", "yhi", "core")
PLANE = ("ylo", "x", "yhi")
RING = 4
ZUP = [(i, (i + 1) % RING) for i in range(RING)]
ZDOWN = [(i, (i - 1) % RING) for i in range(RING)]
SWAP = [(0, 1), (1, 0)]
LINE = 128
LINES = 32
MIB = 1024 * 1024


def attend_kernel(
    lengths_ref,
    q_ref,
    k_ref,
    v_ref,
    nk_ref,
    nv_ref,
    hidden_ref,
    gain_ref,
    pick_ref,
    middle_ref,
    outgoing_ref,
    mixed_ref,
):
    step = pl.program_id(0)
    block, context, _ = k_ref.shape
    scaling = 1.0 / math.sqrt(HDIM)
    first = lax.broadcasted_iota(jnp.int32, (QHEADS, HDIM), 0) < QHEADS // KVHEADS
    position = lax.broadcasted_iota(jnp.int32, (QHEADS, context), 1)
    all_scores = []
    all_own = []
    for i in range(block):
        q = q_ref[i]
        none = jnp.zeros_like(q)
        wide = jnp.concatenate([jnp.where(first, q, none), jnp.where(first, none, q)], axis=1)
        scores = lax.dot_general(
            wide, k_ref[i], (((1,), (1,)), ((), ())), preferred_element_type=jnp.float32
        )
        all_scores.append(
            jnp.where(position < lengths_ref[step * block + i], scores * scaling, -jnp.inf)
        )
        fresh = nk_ref[i : i + 1, :].astype(jnp.float32)
        all_own.append(jnp.sum(wide.astype(jnp.float32) * fresh, axis=1, keepdims=True) * scaling)
    scores = jnp.concatenate(all_scores, axis=0)
    own = jnp.concatenate(all_own, axis=0)
    highest = jnp.maximum(jnp.max(scores, axis=1, keepdims=True), own)
    powers = jnp.exp(scores - highest)
    own_power = jnp.exp(own - highest)
    inverse = 1.0 / (jnp.sum(powers, axis=1, keepdims=True) + own_power)
    probs = (powers * inverse).astype(jnp.bfloat16)
    own_prob = (own_power * inverse).astype(jnp.bfloat16).astype(jnp.float32)
    for i in range(block):
        span = slice(i * QHEADS, (i + 1) * QHEADS)
        mixed = jnp.dot(probs[span], v_ref[i], preferred_element_type=jnp.float32)
        mixed = mixed + own_prob[span] * nv_ref[i : i + 1, :].astype(jnp.float32)
        at = pl.multiple_of((step * block + i) * QHEADS, QHEADS)
        mixed_ref[pl.ds(at, QHEADS), :] = jnp.where(first, mixed[:, :HDIM], mixed[:, HDIM:])

    @pl.when(step == pl.num_programs(0) - 1)
    def _():
        rows, width = middle_ref.shape
        squares = jnp.zeros((rows, HDIM), jnp.float32)
        for head in range(QHEADS):
            cols = slice(head * HDIM, (head + 1) * HDIM)
            middle = hidden_ref[:, cols].astype(jnp.float32) + mixed_ref[
                pl.ds(head, rows, stride=QHEADS), :
            ]
            middle_ref[:, cols] = middle
            squares = squares + middle * middle
        scale = lax.rsqrt(jnp.sum(squares, axis=1, keepdims=True) / width + 1e-06)
        part = 512
        for at in range(0, width, part):
            cols = slice(at, at + part)
            normed = (middle_ref[:, cols] * scale * gain_ref[:, cols]).astype(jnp.bfloat16)
            outgoing_ref[:, cols] = jnp.dot(
                pick_ref[...], normed, preferred_element_type=jnp.float32
            ).astype(jnp.bfloat16)


def attend_call(lengths, queries, keys, values, new_keys, new_values, hidden_states, gain, pick):
    rows, width = hidden_states.shape
    context, features = keys.shape[1:]
    slots = pick.shape[0]
    block = 8
    whole = lambda shape: pl.BlockSpec(shape, lambda i: (0,) * len(shape))
    return pl.pallas_call(
        attend_kernel,
        grid=(rows // block,),
        out_shape=(
            jax.ShapeDtypeStruct((rows, width), jnp.float32),
            jax.ShapeDtypeStruct((slots, width), jnp.bfloat16),
        ),
        in_specs=[
            pl.BlockSpec(memory_space=pltpu.SMEM),
            pl.BlockSpec((block, QHEADS, HDIM), lambda i: (i, 0, 0)),
            pl.BlockSpec((block, context, features), lambda i: (i, 0, 0)),
            pl.BlockSpec((block, context, features), lambda i: (i, 0, 0)),
            pl.BlockSpec((block, features), lambda i: (i, 0)),
            pl.BlockSpec((block, features), lambda i: (i, 0)),
            whole((rows, width)),
            whole((1, width)),
            whole((slots, rows)),
        ],
        out_specs=(whole((rows, width)), whole((slots, width))),
        scratch_shapes=[pltpu.VMEM((rows * QHEADS, HDIM), jnp.float32)],
        compiler_params=pltpu.CompilerParams(vmem_limit_bytes=40 * MIB),
        cost_estimate=pl.CostEstimate(
            flops=2 * rows * 2 * QHEADS * context * features,
            bytes_accessed=64 * MIB,
            transcendentals=rows * QHEADS * context,
        ),
        name="attend",
    )(
        lengths,
        queries.reshape(rows, QHEADS, HDIM),
        keys,
        values,
        new_keys,
        new_values,
        hidden_states,
        gain.reshape(1, width),
        pick,
    )


def spread_piece(piece):
    half = piece.shape[0] // 2
    prev = lax.ppermute(piece, "z", ZUP)
    succ = lax.ppermute(piece, "z", ZDOWN)
    far = [lax.ppermute(prev[:half], "z", ZUP), lax.ppermute(succ[half:], "z", ZDOWN)]
    mine = [piece, prev, succ] + far
    other = [lax.ppermute(part, "core", SWAP) for part in mine]
    return [part.reshape((-1, 8) + part.shape[1:]) for part in mine + other]


def place_copies(place_ref, parts, scratch, sem, kind=None):
    z = place_ref[0]
    core = place_ref[1]
    count = len(parts) // 2
    copies = []
    for index, part in enumerate(parts):
        which = index % count
        c = core if index < count else 1 - core
        zz = lax.rem(z + (0, RING - 1, 1, 2, 2)[which], RING)
        for lo in range(part.shape[0]):
            low = lo if which != 4 else 1
            source = part.at[lo] if kind is None else part.at[lo, :, kind]
            copies.append(pltpu.make_async_copy(source, scratch.at[low, zz, :, c], sem))
    return copies


def hidden_kernel(place_ref, rows_any, *refs):
    parts = refs[:-6]
    out_ref, rows_ref, gate_ref, up_ref, acc_ref, sem = refs[-6:]
    rows_copy = pltpu.make_async_copy(rows_any, rows_ref, sem.at[2])
    rows_copy.start()
    gate_copies = place_copies(place_ref, parts, gate_ref, sem.at[0], 0)
    up_copies = place_copies(place_ref, parts, up_ref, sem.at[1], 1)
    for copy in gate_copies + up_copies:
        copy.start()
    rows_copy.wait()
    for copy in gate_copies:
        copy.wait()
    depth = rows_ref.shape[1]
    width = out_ref.shape[1]
    step = 256

    @pl.loop(0, width // step)
    def _(i):
        cols = pl.ds(pl.multiple_of(i * step, step), step)
        gate = gate_ref[:, :, :, :, :, cols].reshape(depth, step)
        g = jnp.dot(rows_ref[...], gate, preferred_element_type=jnp.float32)
        acc_ref[:, cols] = g / (1.0 + jnp.exp(-g))

    for copy in up_copies:
        copy.wait()

    @pl.loop(0, width // step)
    def _(i):
        cols = pl.ds(pl.multiple_of(i * step, step), step)
        up = up_ref[:, :, :, :, :, cols].reshape(depth, step)
        u = jnp.dot(rows_ref[...], up, preferred_element_type=jnp.float32)
        out_ref[:, cols] = (acc_ref[:, cols] * u).astype(out_ref.dtype)


def hidden_call(place, rows, parts):
    count, depth = rows.shape
    width = parts[0].shape[-1]
    hbm = pl.BlockSpec(memory_space=pl.ANY)
    weight = pltpu.VMEM((2, RING, 8, 2, 32, width), jnp.bfloat16)
    return pl.pallas_call(
        hidden_kernel,
        out_shape=jax.ShapeDtypeStruct((count, width), jnp.bfloat16),
        in_specs=[pl.BlockSpec(memory_space=pltpu.SMEM)]
        + [hbm] * (1 + len(parts)),
        out_specs=pl.BlockSpec(memory_space=pltpu.VMEM),
        scratch_shapes=[
            pltpu.VMEM((count, depth), jnp.bfloat16),
            weight,
            weight,
            pltpu.VMEM((count, width), jnp.float32),
            pltpu.SemaphoreType.DMA((3,)),
        ],
        compiler_params=pltpu.CompilerParams(vmem_limit_bytes=56 * MIB),
        cost_estimate=pl.CostEstimate(
            flops=4 * count * depth * width,
            bytes_accessed=4 * depth * width + 2 * count * depth,
            transcendentals=count * width,
        ),
        name="hidden",
    )(place, rows, *parts)


def project_kernel(place_ref, hidden_ref, *refs):
    parts = refs[:-5]
    out_any, scratch, out_ref, sem, out_sem = refs[-5:]
    copies = place_copies(place_ref, parts, scratch, sem)
    for copy in copies:
        copy.start()
    for copy in copies:
        copy.wait()
    hidden = hidden_ref[...]
    outs = []
    for chunk in range(2 * RING):
        weight = scratch[chunk // RING, chunk % RING].reshape(512, hidden.shape[1])
        cols = slice(chunk * 512, (chunk + 1) * 512)
        out_ref[:, cols] = lax.dot_general(
            hidden, weight, (((1,), (1,)), ((), ())), preferred_element_type=jnp.float32
        ).astype(out_ref.dtype)
        out = pltpu.make_async_copy(out_ref.at[:, cols], out_any.at[:, cols], out_sem.at[chunk])
        out.start()
        outs.append(out)
    for out in outs:
        out.wait()


def project_call(place, hidden, parts):
    count, width = hidden.shape
    depth = 4096
    hbm = pl.BlockSpec(memory_space=pl.ANY)
    return pl.pallas_call(
        project_kernel,
        out_shape=jax.ShapeDtypeStruct((count, depth), jnp.bfloat16),
        in_specs=[
            pl.BlockSpec(memory_space=pltpu.SMEM),
            pl.BlockSpec(memory_space=pltpu.VMEM),
        ]
        + [hbm] * len(parts),
        out_specs=hbm,
        scratch_shapes=[
            pltpu.VMEM((2, RING, 8, 2, 32, width), jnp.bfloat16),
            pltpu.VMEM((count, depth), jnp.bfloat16),
            pltpu.SemaphoreType.DMA,
            pltpu.SemaphoreType.DMA((2 * RING,)),
        ],
        compiler_params=pltpu.CompilerParams(vmem_limit_bytes=56 * MIB),
        cost_estimate=pl.CostEstimate(
            flops=2 * count * depth * width,
            bytes_accessed=2 * depth * width + 2 * count * depth,
            transcendentals=0,
        ),
        name="project",
    )(place, hidden, *parts)


def combine_kernel(weighs_ref, picked_ref, middle_ref, back_ref, layer_ref, parcel_ref, rows_ref):
    step = pl.program_id(0)
    back = back_ref[...]
    rows = layer_ref.shape[0]
    routed = jnp.dot(weighs_ref[...], back, preferred_element_type=jnp.float32)
    routed = routed[:rows] + routed[rows:]
    layer = (middle_ref[...] + routed).astype(jnp.bfloat16)
    layer_ref[...] = layer
    lines = picked_ref.shape[0]
    taken = jnp.dot(picked_ref[...], layer, preferred_element_type=jnp.float32)
    per_step = layer.shape[1] // LINE
    for part in range(per_step):
        rows_ref[pl.ds(step * per_step + part, lines, stride=LINES), :] = taken[
            :, part * LINE : (part + 1) * LINE
        ]

    @pl.when(step == pl.num_programs(0) - 1)
    def _():
        parcel_ref[...] = rows_ref[...].reshape(parcel_ref.shape).astype(parcel_ref.dtype)


def combine_call(weighs, picked, middle, back):
    rows, width = middle.shape
    slots = back.shape[0]
    learners = picked.shape[0]
    step = 512
    whole = lambda shape: pl.BlockSpec(shape, lambda i: (0,) * len(shape))
    column = lambda count: pl.BlockSpec((count, step), lambda i: (0, i))
    return pl.pallas_call(
        combine_kernel,
        grid=(width // step,),
        out_shape=(
            jax.ShapeDtypeStruct((rows, width), jnp.bfloat16),
            jax.ShapeDtypeStruct((learners, LINES, LINE), jnp.bfloat16),
        ),
        in_specs=[
            whole((2 * rows, slots)),
            whole((learners, rows)),
            column(rows),
            column(slots),
        ],
        out_specs=(column(rows), whole((learners, LINES, LINE))),
        scratch_shapes=[pltpu.VMEM((learners * LINES, LINE), jnp.float32)],
        compiler_params=pltpu.CompilerParams(vmem_limit_bytes=16 * MIB),
        name="combine",
    )(weighs, picked, middle, back)


def unpack_kernel(lines_ref, out_ref, rows_ref):
    count = lines_ref.shape[0]
    rows_ref[...] = lines_ref[...].reshape(rows_ref.shape).astype(jnp.float32)
    for part in range(LINES):
        out_ref[:, part * LINE : (part + 1) * LINE] = rows_ref[
            pl.ds(part, count, stride=LINES), :
        ].astype(out_ref.dtype)


def unpack_call(lines):
    count = lines.shape[0]
    vmem = pl.BlockSpec(memory_space=pltpu.VMEM)
    return pl.pallas_call(
        unpack_kernel,
        out_shape=jax.ShapeDtypeStruct((count, LINES * LINE), jnp.bfloat16),
        in_specs=[vmem],
        out_specs=vmem,
        scratch_shapes=[pltpu.VMEM((count * LINES, LINE), jnp.float32)],
        compiler_params=pltpu.CompilerParams(vmem_limit_bytes=16 * MIB),
        name="unpack",
    )(lines)


def shards(
    hidden_states,
    queries,
    key_cache,
    value_cache,
    new_keys,
    new_values,
    cache_lengths,
    norm_gain,
    expert_ids,
    route_weights,
    finished,
    learner_ids,
    gate_weight,
    up_weight,
    down_weight,
):
    experts = 16
    learners = 128
    row_count, model_width = hidden_states.shape
    capacity = row_count // 2
    slots = experts * capacity
    place = jnp.stack([lax.axis_index("z"), lax.axis_index("core")]).astype(jnp.int32)

    to_chip = lambda part: lax.all_to_all(part, PLANE, split_axis=0, concat_axis=0, tiled=True)
    pair = to_chip(jnp.stack([gate_weight, up_weight], axis=1))
    down = to_chip(jnp.swapaxes(down_weight, 1, 2))
    pair_parts = spread_piece(pair)
    down_parts = spread_piece(down)

    expert_range = jnp.arange(experts, dtype=jnp.int32)
    hit_table = expert_ids[:, :, None] == expert_range[None, None, :]
    matched = jnp.any(hit_table, axis=1)
    slot_gate = jnp.sum(jnp.where(hit_table, route_weights[:, :, None], 0.0), axis=1)
    row_range = jnp.arange(row_count, dtype=jnp.int32)
    earlier = row_range[None, :] < row_range[:, None]
    slot_rank = jnp.sum(
        jnp.where(earlier[:, :, None] & matched[None, :, :], 1, 0).astype(jnp.int32), axis=1
    )
    slot_range = jnp.arange(capacity, dtype=jnp.int32)
    chosen = matched[:, :, None] & (slot_rank[:, :, None] == slot_range[None, None, :])
    weigh = jnp.where(chosen, slot_gate[:, :, None], 0.0).reshape(row_count, slots)
    weigh_high = weigh.astype(jnp.bfloat16)
    weigh_low = (weigh - weigh_high.astype(jnp.float32)).astype(jnp.bfloat16)
    weighs = jnp.concatenate([weigh_high, weigh_low], axis=0)
    turned = matched.T[:, None, :] & (slot_rank.T[:, None, :] == slot_range[None, :, None])
    pick = turned.reshape(slots, row_count).astype(jnp.bfloat16)

    finished_rows = finished > 0
    same_target = (learner_ids[:, None] == learner_ids[None, :]) & finished_rows[None, :] & earlier
    learner_rank = jnp.sum(same_target.astype(jnp.int32), axis=1)
    slot_of_row = learner_ids + learner_rank
    slot_span = jnp.arange(learners, dtype=jnp.int32)
    picked = finished_rows[None, :] & (slot_of_row[None, :] == slot_span[:, None])
    picked = picked.astype(jnp.bfloat16)

    queries, weighs, picked, place = lax.optimization_barrier((queries, weighs, picked, place))
    middle, outgoing = attend_call(
        cache_lengths,
        queries,
        key_cache,
        value_cache,
        new_keys,
        new_values,
        hidden_states,
        norm_gain,
        pick,
    )
    outgoing, _, _ = lax.optimization_barrier((outgoing, pair, down))
    received = lax.all_to_all(
        outgoing.reshape(experts, capacity, model_width),
        PLANE,
        split_axis=0,
        concat_axis=0,
        tiled=True,
    ).reshape(slots, model_width)

    hidden = hidden_call(place, received, pair_parts)
    expert_out = project_call(place, hidden, down_parts)
    returned = lax.all_to_all(
        expert_out.reshape(experts, capacity, model_width),
        PLANE,
        split_axis=0,
        concat_axis=0,
        tiled=True,
    ).reshape(slots, model_width)

    layer_out, parcel = combine_call(weighs, picked, middle, returned)
    arrived = lax.all_to_all(parcel, AXES, split_axis=0, concat_axis=0, tiled=True)
    return (layer_out, unpack_call(arrived))


def solution(mesh):
    fine = Mesh(mesh.devices.reshape(2, 4, 4, 2, 2), AXES)
    rows = P(AXES)
    placed = (
        P(AXES, None),
        P(AXES, None),
        P(AXES, None, None),
        P(AXES, None, None),
        P(AXES, None),
        P(AXES, None),
        P(AXES),
        P(),
        P(AXES, None),
        P(AXES, None),
        P(AXES),
        P(AXES),
        P(None, AXES, None),
        P(None, AXES, None),
        P(None, None, AXES),
    )
    return jax.shard_map(
        shards,
        mesh=fine,
        in_specs=placed,
        out_specs=(P(AXES, None), P(AXES, None)),
        check_vma=False,
    )
```

```python
import math

import jax
import jax.numpy as jnp
from jax import lax
from jax.experimental import pallas as pl
from jax.experimental.pallas import tpu as pltpu
from jax.sharding import Mesh
from jax.sharding import PartitionSpec as P

HDIM = 128
QHEADS = 32
KVHEADS = 2

AXES = ("ylo", "z", "x", "yhi", "core")
PLANE = ("ylo", "x", "yhi")
RING = 4
ZUP = [(i, (i + 1) % RING) for i in range(RING)]
ZDOWN = [(i, (i - 1) % RING) for i in range(RING)]
SWAP = [(0, 1), (1, 0)]
STEPS = (0, RING - 1, 1, 2)
NEAR_TAGS = ((0, 0), (1, 0), (2, 0))
FAR_TAGS = ((3, 0), (3, 1))
NEAR_PARTS = 2 * len(NEAR_TAGS)
FAR_PARTS = 2 * len(FAR_TAGS)
LINE = 128
LINES = 32
MIB = 1024 * 1024


def attend_kernel(
    lengths_ref,
    q_ref,
    k_ref,
    v_ref,
    nk_ref,
    nv_ref,
    hidden_ref,
    gain_ref,
    pick_ref,
    middle_ref,
    outgoing_ref,
    mixed_ref,
):
    step = pl.program_id(0)
    block, context, _ = k_ref.shape
    scaling = 1.0 / math.sqrt(HDIM)
    first = lax.broadcasted_iota(jnp.int32, (QHEADS, HDIM), 0) < QHEADS // KVHEADS
    position = lax.broadcasted_iota(jnp.int32, (QHEADS, context), 1)
    all_scores = []
    all_own = []
    for i in range(block):
        q = q_ref[i]
        none = jnp.zeros_like(q)
        wide = jnp.concatenate([jnp.where(first, q, none), jnp.where(first, none, q)], axis=1)
        scores = lax.dot_general(
            wide, k_ref[i], (((1,), (1,)), ((), ())), preferred_element_type=jnp.float32
        )
        all_scores.append(
            jnp.where(position < lengths_ref[step * block + i], scores * scaling, -jnp.inf)
        )
        fresh = nk_ref[i : i + 1, :].astype(jnp.float32)
        all_own.append(jnp.sum(wide.astype(jnp.float32) * fresh, axis=1, keepdims=True) * scaling)
    scores = jnp.concatenate(all_scores, axis=0)
    own = jnp.concatenate(all_own, axis=0)
    highest = jnp.maximum(jnp.max(scores, axis=1, keepdims=True), own)
    powers = jnp.exp(scores - highest)
    own_power = jnp.exp(own - highest)
    inverse = 1.0 / (jnp.sum(powers, axis=1, keepdims=True) + own_power)
    probs = (powers * inverse).astype(jnp.bfloat16)
    own_prob = (own_power * inverse).astype(jnp.bfloat16).astype(jnp.float32)
    for i in range(block):
        span = slice(i * QHEADS, (i + 1) * QHEADS)
        mixed = jnp.dot(probs[span], v_ref[i], preferred_element_type=jnp.float32)
        mixed = mixed + own_prob[span] * nv_ref[i : i + 1, :].astype(jnp.float32)
        at = pl.multiple_of((step * block + i) * QHEADS, QHEADS)
        mixed_ref[pl.ds(at, QHEADS), :] = jnp.where(first, mixed[:, :HDIM], mixed[:, HDIM:])

    @pl.when(step == pl.num_programs(0) - 1)
    def _():
        rows, width = middle_ref.shape
        squares = jnp.zeros((rows, HDIM), jnp.float32)
        for head in range(QHEADS):
            cols = slice(head * HDIM, (head + 1) * HDIM)
            middle = hidden_ref[:, cols].astype(jnp.float32) + mixed_ref[
                pl.ds(head, rows, stride=QHEADS), :
            ]
            middle_ref[:, cols] = middle
            squares = squares + middle * middle
        scale = lax.rsqrt(jnp.sum(squares, axis=1, keepdims=True) / width + 1e-06)
        part = 512
        for at in range(0, width, part):
            cols = slice(at, at + part)
            normed = (middle_ref[:, cols] * scale * gain_ref[:, cols]).astype(jnp.bfloat16)
            outgoing_ref[:, cols] = jnp.dot(
                pick_ref[...], normed, preferred_element_type=jnp.float32
            ).astype(jnp.bfloat16)


def attend_call(lengths, queries, keys, values, new_keys, new_values, hidden_states, gain, pick):
    rows, width = hidden_states.shape
    context, features = keys.shape[1:]
    slots = pick.shape[0]
    block = 8
    whole = lambda shape: pl.BlockSpec(shape, lambda i: (0,) * len(shape))
    return pl.pallas_call(
        attend_kernel,
        grid=(rows // block,),
        out_shape=(
            jax.ShapeDtypeStruct((rows, width), jnp.float32),
            jax.ShapeDtypeStruct((slots, width), jnp.bfloat16),
        ),
        in_specs=[
            pl.BlockSpec(memory_space=pltpu.SMEM),
            pl.BlockSpec((block, QHEADS, HDIM), lambda i: (i, 0, 0)),
            pl.BlockSpec((block, context, features), lambda i: (i, 0, 0)),
            pl.BlockSpec((block, context, features), lambda i: (i, 0, 0)),
            pl.BlockSpec((block, features), lambda i: (i, 0)),
            pl.BlockSpec((block, features), lambda i: (i, 0)),
            whole((rows, width)),
            whole((1, width)),
            whole((slots, rows)),
        ],
        out_specs=(whole((rows, width)), whole((slots, width))),
        scratch_shapes=[pltpu.VMEM((rows * QHEADS, HDIM), jnp.float32)],
        compiler_params=pltpu.CompilerParams(vmem_limit_bytes=40 * MIB),
        cost_estimate=pl.CostEstimate(
            flops=2 * rows * 2 * QHEADS * context * features,
            bytes_accessed=64 * MIB,
            transcendentals=rows * QHEADS * context,
        ),
        name="attend",
    )(
        lengths,
        queries.reshape(rows, QHEADS, HDIM),
        keys,
        values,
        new_keys,
        new_values,
        hidden_states,
        gain.reshape(1, width),
        pick,
    )


def spread_piece(piece):
    half = piece.shape[0] // 2
    prev = lax.ppermute(piece, "z", ZUP)
    succ = lax.ppermute(piece, "z", ZDOWN)
    low_far = lax.ppermute(prev[:half], "z", ZUP)
    high_far = lax.ppermute(succ[half:], "z", ZDOWN)
    return [piece, prev, succ], [low_far, high_far]


def with_other_core(mine):
    parts = mine + [lax.ppermute(part, "core", SWAP) for part in mine]
    return [part.reshape((-1, 8) + part.shape[1:]) for part in parts]


def share_copies(place_ref, parts, tags, lo, target_of, sem, kind=None):
    core = place_ref[1]
    copies = []
    for index, part in enumerate(parts):
        which, first = tags[index % len(tags)]
        if not first <= lo < first + part.shape[0]:
            continue
        c = core if index < len(tags) else 1 - core
        source = part.at[lo - first] if kind is None else part.at[lo - first, :, kind]
        copies.append(pltpu.make_async_copy(source, target_of(which).at[:, c], sem))
    return copies


def share_columns(place_ref, lo, which):
    z = lax.rem(place_ref[0] + STEPS[which], RING)
    return pl.ds(pl.multiple_of(lo * 2048 + z * 512, 512), 512)


def near_kernel(place_ref, rows_any, *refs):
    gate_parts, up_parts = refs[:NEAR_PARTS], refs[NEAR_PARTS : 2 * NEAR_PARTS]
    gate_out, up_out, rows_ref, gate_ref, up_ref, sem = refs[2 * NEAR_PARTS :]
    width = gate_out.shape[1]
    depth = rows_ref.shape[2]
    step = 256
    copies = []
    for lo in range(2):
        group = []
        for which in range(3):
            source = rows_any.at[:, share_columns(place_ref, lo, which)]
            target = rows_ref.at[lo, :, which * 512 : (which + 1) * 512]
            group.append(pltpu.make_async_copy(source, target, sem.at[lo]))
        gate_of = lambda which, lo=lo: gate_ref.at[lo, which]
        up_of = lambda which, lo=lo: up_ref.at[lo, which]
        group += share_copies(place_ref, gate_parts, NEAR_TAGS, lo, gate_of, sem.at[lo])
        group += share_copies(place_ref, up_parts, NEAR_TAGS, lo, up_of, sem.at[lo], 0)
        for copy in group:
            copy.start()
        copies.append(group)
    for lo in range(2):
        for copy in copies[lo]:
            copy.wait()

        @pl.loop(0, width // step)
        def _(i):
            cols = pl.ds(pl.multiple_of(i * step, step), step)
            gate = gate_ref[lo, :, :, :, :, cols].reshape(depth, step)
            up = up_ref[lo, :, :, :, :, cols].reshape(depth, step)
            g = jnp.dot(rows_ref[lo], gate, preferred_element_type=jnp.float32)
            u = jnp.dot(rows_ref[lo], up, preferred_element_type=jnp.float32)
            if lo == 0:
                gate_out[:, cols] = g
                up_out[:, cols] = u
            else:
                gate_out[:, cols] += g
                up_out[:, cols] += u


def near_call(place, rows, gate_parts, up_parts):
    count, depth = rows.shape
    width = gate_parts[0].shape[-1]
    any_place = pl.BlockSpec(memory_space=pl.ANY)
    vmem = pl.BlockSpec(memory_space=pltpu.VMEM)
    weight = pltpu.VMEM((2, 3, 8, 2, 32, width), jnp.bfloat16)
    total = jax.ShapeDtypeStruct((count, width), jnp.float32)
    return pl.pallas_call(
        near_kernel,
        out_shape=(total, total),
        in_specs=[pl.BlockSpec(memory_space=pltpu.SMEM)] + [any_place] * (1 + 2 * NEAR_PARTS),
        out_specs=(vmem, vmem),
        scratch_shapes=[
            pltpu.VMEM((2, count, 3 * 512), jnp.bfloat16),
            weight,
            weight,
            pltpu.SemaphoreType.DMA((2,)),
        ],
        compiler_params=pltpu.CompilerParams(vmem_limit_bytes=52 * MIB),
        cost_estimate=pl.CostEstimate(
            flops=3 * count * depth * width,
            bytes_accessed=3 * depth * width + 2 * count * depth,
            transcendentals=0,
        ),
        name="near",
    )(place, rows, *gate_parts, *up_parts)


def rest_kernel(place_ref, gate_sum, up_sum, rows_any, *refs):
    gate_parts, up_parts = refs[:FAR_PARTS], refs[FAR_PARTS : 2 * FAR_PARTS]
    near_parts = refs[2 * FAR_PARTS : 2 * FAR_PARTS + NEAR_PARTS]
    out_any, rows_ref, gate_ref, up_ref, down_ref, hidden_ref, out_ref, sem, out_sem = refs[
        2 * FAR_PARTS + NEAR_PARTS :
    ]
    width = gate_sum.shape[1]
    step = 256
    copies = []
    for lo in range(2):
        source = rows_any.at[:, share_columns(place_ref, lo, 3)]
        target = rows_ref.at[:, lo * 512 : (lo + 1) * 512]
        copies.append(pltpu.make_async_copy(source, target, sem.at[0]))
        gate_of = lambda which, lo=lo: gate_ref.at[lo]
        up_of = lambda which, lo=lo: up_ref.at[lo]
        copies += share_copies(place_ref, gate_parts, FAR_TAGS, lo, gate_of, sem.at[0])
        copies += share_copies(place_ref, up_parts, FAR_TAGS, lo, up_of, sem.at[0], 0)
    down_copies = []
    for lo in range(2):
        down_of = lambda which, lo=lo: down_ref.at[lo, which]
        group = share_copies(place_ref, near_parts, NEAR_TAGS, lo, down_of, sem.at[1 + lo], 1)
        group += share_copies(place_ref, up_parts, FAR_TAGS, lo, down_of, sem.at[1 + lo], 1)
        down_copies.append(group)
    for copy in copies + down_copies[0] + down_copies[1]:
        copy.start()
    for copy in copies:
        copy.wait()

    @pl.loop(0, width // step)
    def _(i):
        cols = pl.ds(pl.multiple_of(i * step, step), step)
        rows = rows_ref[...]
        gate = gate_ref[:, :, :, :, cols].reshape(1024, step)
        up = up_ref[:, :, :, :, cols].reshape(1024, step)
        g = gate_sum[:, cols] + jnp.dot(rows, gate, preferred_element_type=jnp.float32)
        u = up_sum[:, cols] + jnp.dot(rows, up, preferred_element_type=jnp.float32)
        hidden_ref[:, cols] = (g / (1.0 + jnp.exp(-g)) * u).astype(hidden_ref.dtype)

    outs = []
    for lo in range(2):
        for copy in down_copies[lo]:
            copy.wait()
        for which in range(RING):
            chunk = lo * RING + which
            weight = down_ref[lo, which].reshape(512, width)
            out_ref[chunk] = lax.dot_general(
                hidden_ref[...],
                weight,
                (((1,), (1,)), ((), ())),
                preferred_element_type=jnp.float32,
            ).astype(out_ref.dtype)
            target = out_any.at[:, share_columns(place_ref, lo, which)]
            out = pltpu.make_async_copy(out_ref.at[chunk], target, out_sem.at[chunk])
            out.start()
            outs.append(out)
    for out in outs:
        out.wait()


def rest_call(place, sums, rows, gate_parts, up_parts, near_parts):
    count, depth = rows.shape
    width = gate_parts[0].shape[-1]
    any_place = pl.BlockSpec(memory_space=pl.ANY)
    vmem = pl.BlockSpec(memory_space=pltpu.VMEM)
    weight = pltpu.VMEM((2, 8, 2, 32, width), jnp.bfloat16)
    return pl.pallas_call(
        rest_kernel,
        out_shape=jax.ShapeDtypeStruct((count, depth), jnp.bfloat16),
        in_specs=[pl.BlockSpec(memory_space=pltpu.SMEM), vmem, vmem]
        + [any_place] * (1 + 2 * FAR_PARTS + NEAR_PARTS),
        out_specs=any_place,
        scratch_shapes=[
            pltpu.VMEM((count, 1024), jnp.bfloat16),
            weight,
            weight,
            pltpu.VMEM((2, RING, 8, 2, 32, width), jnp.bfloat16),
            pltpu.VMEM((count, width), jnp.bfloat16),
            pltpu.VMEM((2 * RING, count, 512), jnp.bfloat16),
            pltpu.SemaphoreType.DMA((3,)),
            pltpu.SemaphoreType.DMA((2 * RING,)),
        ],
        compiler_params=pltpu.CompilerParams(vmem_limit_bytes=52 * MIB),
        cost_estimate=pl.CostEstimate(
            flops=3 * count * depth * width,
            bytes_accessed=3 * depth * width + 2 * count * depth,
            transcendentals=count * width,
        ),
        name="rest",
    )(place, *sums, rows, *gate_parts, *up_parts, *near_parts)


def combine_kernel(weighs_ref, picked_ref, middle_ref, back_ref, layer_ref, parcel_ref, rows_ref):
    step = pl.program_id(0)
    back = back_ref[...]
    rows = layer_ref.shape[0]
    routed = jnp.dot(weighs_ref[...], back, preferred_element_type=jnp.float32)
    routed = routed[:rows] + routed[rows:]
    layer = (middle_ref[...] + routed).astype(jnp.bfloat16)
    layer_ref[...] = layer
    lines = picked_ref.shape[0]
    taken = jnp.dot(picked_ref[...], layer, preferred_element_type=jnp.float32)
    per_step = layer.shape[1] // LINE
    for part in range(per_step):
        rows_ref[pl.ds(step * per_step + part, lines, stride=LINES), :] = taken[
            :, part * LINE : (part + 1) * LINE
        ]

    @pl.when(step == pl.num_programs(0) - 1)
    def _():
        parcel_ref[...] = rows_ref[...].reshape(parcel_ref.shape).astype(parcel_ref.dtype)


def combine_call(weighs, picked, middle, back):
    rows, width = middle.shape
    slots = back.shape[0]
    learners = picked.shape[0]
    step = 512
    whole = lambda shape: pl.BlockSpec(shape, lambda i: (0,) * len(shape))
    column = lambda count: pl.BlockSpec((count, step), lambda i: (0, i))
    return pl.pallas_call(
        combine_kernel,
        grid=(width // step,),
        out_shape=(
            jax.ShapeDtypeStruct((rows, width), jnp.bfloat16),
            jax.ShapeDtypeStruct((learners, LINES, LINE), jnp.bfloat16),
        ),
        in_specs=[
            whole((2 * rows, slots)),
            whole((learners, rows)),
            column(rows),
            column(slots),
        ],
        out_specs=(column(rows), whole((learners, LINES, LINE))),
        scratch_shapes=[pltpu.VMEM((learners * LINES, LINE), jnp.float32)],
        compiler_params=pltpu.CompilerParams(vmem_limit_bytes=16 * MIB),
        name="combine",
    )(weighs, picked, middle, back)


def unpack_kernel(lines_ref, out_ref, rows_ref):
    count = lines_ref.shape[0]
    rows_ref[...] = lines_ref[...].reshape(rows_ref.shape).astype(jnp.float32)
    for part in range(LINES):
        out_ref[:, part * LINE : (part + 1) * LINE] = rows_ref[
            pl.ds(part, count, stride=LINES), :
        ].astype(out_ref.dtype)


def unpack_call(lines):
    count = lines.shape[0]
    vmem = pl.BlockSpec(memory_space=pltpu.VMEM)
    return pl.pallas_call(
        unpack_kernel,
        out_shape=jax.ShapeDtypeStruct((count, LINES * LINE), jnp.bfloat16),
        in_specs=[vmem],
        out_specs=vmem,
        scratch_shapes=[pltpu.VMEM((count * LINES, LINE), jnp.float32)],
        compiler_params=pltpu.CompilerParams(vmem_limit_bytes=16 * MIB),
        name="unpack",
    )(lines)


def shards(
    hidden_states,
    queries,
    key_cache,
    value_cache,
    new_keys,
    new_values,
    cache_lengths,
    norm_gain,
    expert_ids,
    route_weights,
    finished,
    learner_ids,
    gate_weight,
    up_weight,
    down_weight,
):
    experts = 16
    learners = 128
    row_count, model_width = hidden_states.shape
    capacity = row_count // 2
    slots = experts * capacity
    place = jnp.stack([lax.axis_index("z"), lax.axis_index("core")]).astype(jnp.int32)

    to_chip = lambda part: lax.all_to_all(part, PLANE, split_axis=0, concat_axis=0, tiled=True)
    gate = to_chip(gate_weight)
    pair = jnp.stack([up_weight, jnp.swapaxes(down_weight, 1, 2)], axis=1)
    pair, queries, gate = lax.optimization_barrier((pair, queries, gate))
    pair = to_chip(pair)
    gate_near, gate_far = spread_piece(gate)

    expert_range = jnp.arange(experts, dtype=jnp.int32)
    hit_table = expert_ids[:, :, None] == expert_range[None, None, :]
    matched = jnp.any(hit_table, axis=1)
    slot_gate = jnp.sum(jnp.where(hit_table, route_weights[:, :, None], 0.0), axis=1)
    row_range = jnp.arange(row_count, dtype=jnp.int32)
    earlier = row_range[None, :] < row_range[:, None]
    slot_rank = jnp.sum(
        jnp.where(earlier[:, :, None] & matched[None, :, :], 1, 0).astype(jnp.int32), axis=1
    )
    slot_range = jnp.arange(capacity, dtype=jnp.int32)
    chosen = matched[:, :, None] & (slot_rank[:, :, None] == slot_range[None, None, :])
    weigh = jnp.where(chosen, slot_gate[:, :, None], 0.0).reshape(row_count, slots)
    weigh_high = weigh.astype(jnp.bfloat16)
    weigh_low = (weigh - weigh_high.astype(jnp.float32)).astype(jnp.bfloat16)
    weighs = jnp.concatenate([weigh_high, weigh_low], axis=0)
    turned = matched.T[:, None, :] & (slot_rank.T[:, None, :] == slot_range[None, :, None])
    pick = turned.reshape(slots, row_count).astype(jnp.bfloat16)

    finished_rows = finished > 0
    same_target = (learner_ids[:, None] == learner_ids[None, :]) & finished_rows[None, :] & earlier
    learner_rank = jnp.sum(same_target.astype(jnp.int32), axis=1)
    slot_of_row = learner_ids + learner_rank
    slot_span = jnp.arange(learners, dtype=jnp.int32)
    picked = finished_rows[None, :] & (slot_of_row[None, :] == slot_span[:, None])
    picked = picked.astype(jnp.bfloat16)

    queries, weighs, picked, place = lax.optimization_barrier((queries, weighs, picked, place))
    middle, outgoing = attend_call(
        cache_lengths,
        queries,
        key_cache,
        value_cache,
        new_keys,
        new_values,
        hidden_states,
        norm_gain,
        pick,
    )
    pair, outgoing, _, _ = lax.optimization_barrier((pair, outgoing, gate_near[1], gate_near[2]))
    pair_near, pair_far = spread_piece(pair)
    received = lax.all_to_all(
        outgoing.reshape(experts, capacity, model_width),
        PLANE,
        split_axis=0,
        concat_axis=0,
        tiled=True,
    ).reshape(slots, model_width)

    pair_near = with_other_core(pair_near)
    sums = near_call(place, received, with_other_core(gate_near), pair_near)
    gate_far = with_other_core(gate_far)
    low_far, high_far, *sums = lax.optimization_barrier((*pair_far, *sums))
    pair_far = with_other_core([low_far, high_far])
    expert_out = rest_call(place, sums, received, gate_far, pair_far, pair_near)
    returned = lax.all_to_all(
        expert_out.reshape(experts, capacity, model_width),
        PLANE,
        split_axis=0,
        concat_axis=0,
        tiled=True,
    ).reshape(slots, model_width)

    layer_out, parcel = combine_call(weighs, picked, middle, returned)
    arrived = lax.all_to_all(parcel, AXES, split_axis=0, concat_axis=0, tiled=True)
    return (layer_out, unpack_call(arrived))


def solution(mesh):
    fine = Mesh(mesh.devices.reshape(2, 4, 4, 2, 2), AXES)
    rows = P(AXES)
    placed = (
        P(AXES, None),
        P(AXES, None),
        P(AXES, None, None),
        P(AXES, None, None),
        P(AXES, None),
        P(AXES, None),
        P(AXES),
        P(),
        P(AXES, None),
        P(AXES, None),
        P(AXES),
        P(AXES),
        P(None, AXES, None),
        P(None, AXES, None),
        P(None, None, AXES),
    )
    return jax.shard_map(
        shards,
        mesh=fine,
        in_specs=placed,
        out_specs=(P(AXES, None), P(AXES, None)),
        check_vma=False,
    )
```

```python
import math

import jax
import jax.numpy as jnp
from jax import lax
from jax.experimental import pallas as pl
from jax.experimental.pallas import tpu as pltpu
from jax.sharding import Mesh
from jax.sharding import PartitionSpec as P

HDIM = 128
QHEADS = 32
KVHEADS = 2

AXES = ("ylo", "z", "x", "yhi", "core")
PLANE = ("ylo", "x", "yhi")
RING = 4
ZUP = [(i, (i + 1) % RING) for i in range(RING)]
ZDOWN = [(i, (i - 1) % RING) for i in range(RING)]
SWAP = [(0, 1), (1, 0)]
STEPS = (0, RING - 1, 1, 2)
NEAR_TAGS = ((0, 0), (1, 0), (2, 0))
FAR_TAGS = ((3, 0), (3, 1))
NEAR_PARTS = 2 * len(NEAR_TAGS)
FAR_PARTS = 2 * len(FAR_TAGS)
LINE = 128
LINES = 32
MIB = 1024 * 1024


def attend_kernel(
    lengths_ref,
    q_ref,
    k_ref,
    v_ref,
    nk_ref,
    nv_ref,
    hidden_ref,
    gain_ref,
    pick_ref,
    middle_ref,
    outgoing_ref,
    mixed_ref,
):
    step = pl.program_id(0)
    block, context, _ = k_ref.shape
    scaling = 1.0 / math.sqrt(HDIM)
    first = lax.broadcasted_iota(jnp.int32, (QHEADS, HDIM), 0) < QHEADS // KVHEADS
    position = lax.broadcasted_iota(jnp.int32, (QHEADS, context), 1)
    all_scores = []
    all_own = []
    for i in range(block):
        q = q_ref[i]
        none = jnp.zeros_like(q)
        wide = jnp.concatenate([jnp.where(first, q, none), jnp.where(first, none, q)], axis=1)
        scores = lax.dot_general(
            wide, k_ref[i], (((1,), (1,)), ((), ())), preferred_element_type=jnp.float32
        )
        all_scores.append(
            jnp.where(position < lengths_ref[step * block + i], scores * scaling, -jnp.inf)
        )
        fresh = nk_ref[i : i + 1, :].astype(jnp.float32)
        all_own.append(jnp.sum(wide.astype(jnp.float32) * fresh, axis=1, keepdims=True) * scaling)
    scores = jnp.concatenate(all_scores, axis=0)
    own = jnp.concatenate(all_own, axis=0)
    highest = jnp.maximum(jnp.max(scores, axis=1, keepdims=True), own)
    powers = jnp.exp(scores - highest)
    own_power = jnp.exp(own - highest)
    inverse = 1.0 / (jnp.sum(powers, axis=1, keepdims=True) + own_power)
    probs = (powers * inverse).astype(jnp.bfloat16)
    own_prob = (own_power * inverse).astype(jnp.bfloat16).astype(jnp.float32)
    for i in range(block):
        span = slice(i * QHEADS, (i + 1) * QHEADS)
        mixed = jnp.dot(probs[span], v_ref[i], preferred_element_type=jnp.float32)
        mixed = mixed + own_prob[span] * nv_ref[i : i + 1, :].astype(jnp.float32)
        at = pl.multiple_of((step * block + i) * QHEADS, QHEADS)
        mixed_ref[pl.ds(at, QHEADS), :] = jnp.where(first, mixed[:, :HDIM], mixed[:, HDIM:])

    @pl.when(step == pl.num_programs(0) - 1)
    def _():
        rows, width = middle_ref.shape
        squares = jnp.zeros((rows, HDIM), jnp.float32)
        for head in range(QHEADS):
            cols = slice(head * HDIM, (head + 1) * HDIM)
            middle = hidden_ref[:, cols].astype(jnp.float32) + mixed_ref[
                pl.ds(head, rows, stride=QHEADS), :
            ]
            middle_ref[:, cols] = middle
            squares = squares + middle * middle
        scale = lax.rsqrt(jnp.sum(squares, axis=1, keepdims=True) / width + 1e-06)
        part = 512
        for at in range(0, width, part):
            cols = slice(at, at + part)
            normed = (middle_ref[:, cols] * scale * gain_ref[:, cols]).astype(jnp.bfloat16)
            outgoing_ref[:, cols] = jnp.dot(
                pick_ref[...], normed, preferred_element_type=jnp.float32
            ).astype(jnp.bfloat16)


def attend_call(lengths, queries, keys, values, new_keys, new_values, hidden_states, gain, pick):
    rows, width = hidden_states.shape
    context, features = keys.shape[1:]
    slots = pick.shape[0]
    block = 8
    whole = lambda shape: pl.BlockSpec(shape, lambda i: (0,) * len(shape))
    return pl.pallas_call(
        attend_kernel,
        grid=(rows // block,),
        out_shape=(
            jax.ShapeDtypeStruct((rows, width), jnp.float32),
            jax.ShapeDtypeStruct((slots, width), jnp.bfloat16),
        ),
        in_specs=[
            pl.BlockSpec(memory_space=pltpu.SMEM),
            pl.BlockSpec((block, QHEADS, HDIM), lambda i: (i, 0, 0)),
            pl.BlockSpec((block, context, features), lambda i: (i, 0, 0)),
            pl.BlockSpec((block, context, features), lambda i: (i, 0, 0)),
            pl.BlockSpec((block, features), lambda i: (i, 0)),
            pl.BlockSpec((block, features), lambda i: (i, 0)),
            whole((rows, width)),
            whole((1, width)),
            whole((slots, rows)),
        ],
        out_specs=(whole((rows, width)), whole((slots, width))),
        scratch_shapes=[pltpu.VMEM((rows * QHEADS, HDIM), jnp.float32)],
        compiler_params=pltpu.CompilerParams(vmem_limit_bytes=40 * MIB),
        cost_estimate=pl.CostEstimate(
            flops=2 * rows * 2 * QHEADS * context * features,
            bytes_accessed=64 * MIB,
            transcendentals=rows * QHEADS * context,
        ),
        name="attend",
    )(
        lengths,
        queries.reshape(rows, QHEADS, HDIM),
        keys,
        values,
        new_keys,
        new_values,
        hidden_states,
        gain.reshape(1, width),
        pick,
    )


def spread_piece(piece):
    half = piece.shape[0] // 2
    prev = lax.ppermute(piece, "z", ZUP)
    succ = lax.ppermute(piece, "z", ZDOWN)
    low_far = lax.ppermute(prev[:half], "z", ZUP)
    high_far = lax.ppermute(succ[half:], "z", ZDOWN)
    return [piece, prev, succ], [low_far, high_far]


def with_other_core(mine):
    parts = mine + [lax.ppermute(part, "core", SWAP) for part in mine]
    return [part.reshape((-1, 8) + part.shape[1:]) for part in parts]


def share_copies(place_ref, parts, tags, lo, target_of, sem, kind=None):
    core = place_ref[1]
    copies = []
    for index, part in enumerate(parts):
        which, first = tags[index % len(tags)]
        if not first <= lo < first + part.shape[0]:
            continue
        c = core if index < len(tags) else 1 - core
        source = part.at[lo - first] if kind is None else part.at[lo - first, :, kind]
        copies.append(pltpu.make_async_copy(source, target_of(which).at[:, c], sem))
    return copies


def share_columns(place_ref, lo, which):
    z = lax.rem(place_ref[0] + STEPS[which], RING)
    return pl.ds(pl.multiple_of(lo * 2048 + z * 512, 512), 512)


def near_kernel(place_ref, rows_any, *refs):
    gate_parts, up_parts = refs[:NEAR_PARTS], refs[NEAR_PARTS : 2 * NEAR_PARTS]
    gate_out, up_out, rows_ref, gate_ref, up_ref, sem = refs[2 * NEAR_PARTS :]
    width = gate_out.shape[1]
    depth = rows_ref.shape[2]
    step = 256
    copies = []
    for lo in range(2):
        group = []
        for which in range(3):
            source = rows_any.at[:, share_columns(place_ref, lo, which)]
            target = rows_ref.at[lo, :, which * 512 : (which + 1) * 512]
            group.append(pltpu.make_async_copy(source, target, sem.at[lo]))
        gate_of = lambda which, lo=lo: gate_ref.at[lo, which]
        up_of = lambda which, lo=lo: up_ref.at[lo, which]
        group += share_copies(place_ref, gate_parts, NEAR_TAGS, lo, gate_of, sem.at[lo])
        group += share_copies(place_ref, up_parts, NEAR_TAGS, lo, up_of, sem.at[lo], 0)
        for copy in group:
            copy.start()
        copies.append(group)
    for lo in range(2):
        for copy in copies[lo]:
            copy.wait()

        @pl.loop(0, width // step)
        def _(i):
            cols = pl.ds(pl.multiple_of(i * step, step), step)
            gate = gate_ref[lo, :, :, :, :, cols].reshape(depth, step)
            up = up_ref[lo, :, :, :, :, cols].reshape(depth, step)
            g = jnp.dot(rows_ref[lo], gate, preferred_element_type=jnp.float32)
            u = jnp.dot(rows_ref[lo], up, preferred_element_type=jnp.float32)
            if lo == 0:
                gate_out[:, cols] = g
                up_out[:, cols] = u
            else:
                gate_out[:, cols] += g
                up_out[:, cols] += u


def near_call(place, rows, gate_parts, up_parts):
    count, depth = rows.shape
    width = gate_parts[0].shape[-1]
    any_place = pl.BlockSpec(memory_space=pl.ANY)
    vmem = pl.BlockSpec(memory_space=pltpu.VMEM)
    weight = pltpu.VMEM((2, 3, 8, 2, 32, width), jnp.bfloat16)
    total = jax.ShapeDtypeStruct((count, width), jnp.float32)
    return pl.pallas_call(
        near_kernel,
        out_shape=(total, total),
        in_specs=[pl.BlockSpec(memory_space=pltpu.SMEM)] + [any_place] * (1 + 2 * NEAR_PARTS),
        out_specs=(vmem, vmem),
        scratch_shapes=[
            pltpu.VMEM((2, count, 3 * 512), jnp.bfloat16),
            weight,
            weight,
            pltpu.SemaphoreType.DMA((2,)),
        ],
        compiler_params=pltpu.CompilerParams(vmem_limit_bytes=52 * MIB),
        cost_estimate=pl.CostEstimate(
            flops=3 * count * depth * width,
            bytes_accessed=3 * depth * width + 2 * count * depth,
            transcendentals=0,
        ),
        name="near",
    )(place, rows, *gate_parts, *up_parts)


def rest_kernel(place_ref, gate_sum, up_sum, rows_any, *refs):
    gate_parts, up_parts = refs[:FAR_PARTS], refs[FAR_PARTS : 2 * FAR_PARTS]
    near_parts = refs[2 * FAR_PARTS : 2 * FAR_PARTS + NEAR_PARTS]
    out_any, rows_ref, gate_ref, up_ref, down_ref, hidden_ref, out_ref, sem, out_sem = refs[
        2 * FAR_PARTS + NEAR_PARTS :
    ]
    width = gate_sum.shape[1]
    step = 256
    copies = []
    for lo in range(2):
        source = rows_any.at[:, share_columns(place_ref, lo, 3)]
        target = rows_ref.at[:, lo * 512 : (lo + 1) * 512]
        copies.append(pltpu.make_async_copy(source, target, sem.at[0]))
        gate_of = lambda which, lo=lo: gate_ref.at[lo]
        up_of = lambda which, lo=lo: up_ref.at[lo]
        copies += share_copies(place_ref, gate_parts, FAR_TAGS, lo, gate_of, sem.at[0])
        copies += share_copies(place_ref, up_parts, FAR_TAGS, lo, up_of, sem.at[0], 0)
    down_copies = []
    for lo in range(2):
        down_of = lambda which, lo=lo: down_ref.at[lo, which]
        group = share_copies(place_ref, near_parts, NEAR_TAGS, lo, down_of, sem.at[1 + lo], 1)
        group += share_copies(place_ref, up_parts, FAR_TAGS, lo, down_of, sem.at[1 + lo], 1)
        down_copies.append(group)
    for copy in copies + down_copies[0] + down_copies[1]:
        copy.start()
    for copy in copies:
        copy.wait()

    @pl.loop(0, width // step)
    def _(i):
        cols = pl.ds(pl.multiple_of(i * step, step), step)
        rows = rows_ref[...]
        gate = gate_ref[:, :, :, :, cols].reshape(1024, step)
        up = up_ref[:, :, :, :, cols].reshape(1024, step)
        g = gate_sum[:, cols] + jnp.dot(rows, gate, preferred_element_type=jnp.float32)
        u = up_sum[:, cols] + jnp.dot(rows, up, preferred_element_type=jnp.float32)
        hidden_ref[:, cols] = (g / (1.0 + jnp.exp(-g)) * u).astype(hidden_ref.dtype)

    outs = []
    for lo in range(2):
        for copy in down_copies[lo]:
            copy.wait()
        for which in range(RING):
            chunk = lo * RING + which
            weight = down_ref[lo, which].reshape(512, width)
            out_ref[chunk] = lax.dot_general(
                hidden_ref[...],
                weight,
                (((1,), (1,)), ((), ())),
                preferred_element_type=jnp.float32,
            ).astype(out_ref.dtype)
            target = out_any.at[:, share_columns(place_ref, lo, which)]
            out = pltpu.make_async_copy(out_ref.at[chunk], target, out_sem.at[chunk])
            out.start()
            outs.append(out)
    for out in outs:
        out.wait()


def rest_call(place, sums, rows, gate_parts, up_parts, near_parts):
    count, depth = rows.shape
    width = gate_parts[0].shape[-1]
    any_place = pl.BlockSpec(memory_space=pl.ANY)
    vmem = pl.BlockSpec(memory_space=pltpu.VMEM)
    weight = pltpu.VMEM((2, 8, 2, 32, width), jnp.bfloat16)
    return pl.pallas_call(
        rest_kernel,
        out_shape=jax.ShapeDtypeStruct((count, depth), jnp.bfloat16),
        in_specs=[pl.BlockSpec(memory_space=pltpu.SMEM), vmem, vmem]
        + [any_place] * (1 + 2 * FAR_PARTS + NEAR_PARTS),
        out_specs=any_place,
        scratch_shapes=[
            pltpu.VMEM((count, 1024), jnp.bfloat16),
            weight,
            weight,
            pltpu.VMEM((2, RING, 8, 2, 32, width), jnp.bfloat16),
            pltpu.VMEM((count, width), jnp.bfloat16),
            pltpu.VMEM((2 * RING, count, 512), jnp.bfloat16),
            pltpu.SemaphoreType.DMA((3,)),
            pltpu.SemaphoreType.DMA((2 * RING,)),
        ],
        compiler_params=pltpu.CompilerParams(vmem_limit_bytes=52 * MIB),
        cost_estimate=pl.CostEstimate(
            flops=3 * count * depth * width,
            bytes_accessed=3 * depth * width + 2 * count * depth,
            transcendentals=count * width,
        ),
        name="rest",
    )(place, *sums, rows, *gate_parts, *up_parts, *near_parts)


def combine_kernel(weighs_ref, picked_ref, middle_ref, back_ref, layer_ref, parcel_ref, rows_ref):
    step = pl.program_id(0)
    back = back_ref[...]
    rows = layer_ref.shape[0]
    routed = jnp.dot(weighs_ref[...], back, preferred_element_type=jnp.float32)
    routed = routed[:rows] + routed[rows:]
    layer = (middle_ref[...] + routed).astype(jnp.bfloat16)
    layer_ref[...] = layer
    lines = picked_ref.shape[0]
    taken = jnp.dot(picked_ref[...], layer, preferred_element_type=jnp.float32)
    per_step = layer.shape[1] // LINE
    for part in range(per_step):
        rows_ref[pl.ds(step * per_step + part, lines, stride=LINES), :] = taken[
            :, part * LINE : (part + 1) * LINE
        ]

    @pl.when(step == pl.num_programs(0) - 1)
    def _():
        parcel_ref[...] = rows_ref[...].reshape(parcel_ref.shape).astype(parcel_ref.dtype)


def combine_call(weighs, picked, middle, back):
    rows, width = middle.shape
    slots = back.shape[0]
    learners = picked.shape[0]
    step = 1024
    whole = lambda shape: pl.BlockSpec(shape, lambda i: (0,) * len(shape))
    column = lambda count: pl.BlockSpec((count, step), lambda i: (0, i))
    return pl.pallas_call(
        combine_kernel,
        grid=(width // step,),
        out_shape=(
            jax.ShapeDtypeStruct((rows, width), jnp.bfloat16),
            jax.ShapeDtypeStruct((learners, LINES, LINE), jnp.bfloat16),
        ),
        in_specs=[
            whole((2 * rows, slots)),
            whole((learners, rows)),
            column(rows),
            column(slots),
        ],
        out_specs=(column(rows), whole((learners, LINES, LINE))),
        scratch_shapes=[pltpu.VMEM((learners * LINES, LINE), jnp.float32)],
        compiler_params=pltpu.CompilerParams(vmem_limit_bytes=16 * MIB),
        name="combine",
    )(weighs, picked, middle, back)


def unpack_kernel(lines_ref, out_ref, rows_ref):
    count = lines_ref.shape[0]
    rows_ref[...] = lines_ref[...].reshape(rows_ref.shape).astype(jnp.float32)
    for part in range(LINES):
        out_ref[:, part * LINE : (part + 1) * LINE] = rows_ref[
            pl.ds(part, count, stride=LINES), :
        ].astype(out_ref.dtype)


def unpack_call(lines):
    count = lines.shape[0]
    block = count // 4
    return pl.pallas_call(
        unpack_kernel,
        grid=(4,),
        out_shape=jax.ShapeDtypeStruct((count, LINES * LINE), jnp.bfloat16),
        in_specs=[pl.BlockSpec((block, LINES, LINE), lambda i: (i, 0, 0))],
        out_specs=pl.BlockSpec((block, LINES * LINE), lambda i: (i, 0)),
        scratch_shapes=[pltpu.VMEM((block * LINES, LINE), jnp.float32)],
        compiler_params=pltpu.CompilerParams(vmem_limit_bytes=16 * MIB),
        name="unpack",
    )(lines)


def shards(
    hidden_states,
    queries,
    key_cache,
    value_cache,
    new_keys,
    new_values,
    cache_lengths,
    norm_gain,
    expert_ids,
    route_weights,
    finished,
    learner_ids,
    gate_weight,
    up_weight,
    down_weight,
):
    experts = 16
    learners = 128
    row_count, model_width = hidden_states.shape
    capacity = row_count // 2
    slots = experts * capacity
    place = jnp.stack([lax.axis_index("z"), lax.axis_index("core")]).astype(jnp.int32)

    to_chip = lambda part: lax.all_to_all(part, PLANE, split_axis=0, concat_axis=0, tiled=True)
    gate = to_chip(gate_weight)
    pair = jnp.stack([up_weight, jnp.swapaxes(down_weight, 1, 2)], axis=1)
    pair, queries, gate = lax.optimization_barrier((pair, queries, gate))
    pair = to_chip(pair)
    gate_near, gate_far = spread_piece(gate)

    expert_range = jnp.arange(experts, dtype=jnp.int32)
    hit_table = expert_ids[:, :, None] == expert_range[None, None, :]
    matched = jnp.any(hit_table, axis=1)
    slot_gate = jnp.sum(jnp.where(hit_table, route_weights[:, :, None], 0.0), axis=1)
    row_range = jnp.arange(row_count, dtype=jnp.int32)
    earlier = row_range[None, :] < row_range[:, None]
    slot_rank = jnp.sum(
        jnp.where(earlier[:, :, None] & matched[None, :, :], 1, 0).astype(jnp.int32), axis=1
    )
    slot_range = jnp.arange(capacity, dtype=jnp.int32)
    chosen = matched[:, :, None] & (slot_rank[:, :, None] == slot_range[None, None, :])
    weigh = jnp.where(chosen, slot_gate[:, :, None], 0.0).reshape(row_count, slots)
    weigh_high = weigh.astype(jnp.bfloat16)
    weigh_low = (weigh - weigh_high.astype(jnp.float32)).astype(jnp.bfloat16)
    weighs = jnp.concatenate([weigh_high, weigh_low], axis=0)
    turned = matched.T[:, None, :] & (slot_rank.T[:, None, :] == slot_range[None, :, None])
    pick = turned.reshape(slots, row_count).astype(jnp.bfloat16)

    finished_rows = finished > 0
    same_target = (learner_ids[:, None] == learner_ids[None, :]) & finished_rows[None, :] & earlier
    learner_rank = jnp.sum(same_target.astype(jnp.int32), axis=1)
    slot_of_row = learner_ids + learner_rank
    slot_span = jnp.arange(learners, dtype=jnp.int32)
    picked = finished_rows[None, :] & (slot_of_row[None, :] == slot_span[:, None])
    picked = picked.astype(jnp.bfloat16)

    queries, weighs, picked, place = lax.optimization_barrier((queries, weighs, picked, place))
    middle, outgoing = attend_call(
        cache_lengths,
        queries,
        key_cache,
        value_cache,
        new_keys,
        new_values,
        hidden_states,
        norm_gain,
        pick,
    )
    pair, outgoing, _, _ = lax.optimization_barrier((pair, outgoing, gate_near[1], gate_near[2]))
    pair_near, pair_far = spread_piece(pair)
    received = lax.all_to_all(
        outgoing.reshape(experts, capacity, model_width),
        PLANE,
        split_axis=0,
        concat_axis=0,
        tiled=True,
    ).reshape(slots, model_width)

    pair_near = with_other_core(pair_near)
    sums = near_call(place, received, with_other_core(gate_near), pair_near)
    gate_far = with_other_core(gate_far)
    low_far, high_far, *sums = lax.optimization_barrier((*pair_far, *sums))
    pair_far = with_other_core([low_far, high_far])
    expert_out = rest_call(place, sums, received, gate_far, pair_far, pair_near)
    returned = lax.all_to_all(
        expert_out.reshape(experts, capacity, model_width),
        PLANE,
        split_axis=0,
        concat_axis=0,
        tiled=True,
    ).reshape(slots, model_width)

    layer_out, parcel = combine_call(weighs, picked, middle, returned)
    arrived = lax.all_to_all(parcel, AXES, split_axis=0, concat_axis=0, tiled=True)
    return (layer_out, unpack_call(arrived))


def solution(mesh):
    fine = Mesh(mesh.devices.reshape(2, 4, 4, 2, 2), AXES)
    rows = P(AXES)
    placed = (
        P(AXES, None),
        P(AXES, None),
        P(AXES, None, None),
        P(AXES, None, None),
        P(AXES, None),
        P(AXES, None),
        P(AXES),
        P(),
        P(AXES, None),
        P(AXES, None),
        P(AXES),
        P(AXES),
        P(None, AXES, None),
        P(None, AXES, None),
        P(None, None, AXES),
    )
    return jax.shard_map(
        shards,
        mesh=fine,
        in_specs=placed,
        out_specs=(P(AXES, None), P(AXES, None)),
        check_vma=False,
    )
```

```python
import math

import jax
import jax.numpy as jnp
from jax import lax
from jax.experimental import pallas as pl
from jax.experimental.pallas import tpu as pltpu
from jax.sharding import Mesh
from jax.sharding import PartitionSpec as P

HDIM = 128
QHEADS = 32
KVHEADS = 2

AXES = ("ylo", "z", "x", "yhi", "core")
PLANE = ("ylo", "x", "yhi")
RING = 4
ZUP = [(i, (i + 1) % RING) for i in range(RING)]
ZDOWN = [(i, (i - 1) % RING) for i in range(RING)]
SWAP = [(0, 1), (1, 0)]
STEPS = (0, RING - 1, 1, 2)
NEAR_TAGS = ((0, 0), (1, 0), (2, 0))
FAR_TAGS = ((3, 0), (3, 1))
NEAR_PARTS = 2 * len(NEAR_TAGS)
FAR_PARTS = 2 * len(FAR_TAGS)
LINE = 128
LINES = 32
MIB = 1024 * 1024


def attend_kernel(
    lengths_ref,
    q_ref,
    k_ref,
    v_ref,
    nk_ref,
    nv_ref,
    hidden_ref,
    gain_ref,
    pick_ref,
    middle_ref,
    outgoing_ref,
    mixed_ref,
):
    step = pl.program_id(0)
    block, context, _ = k_ref.shape
    scaling = 1.0 / math.sqrt(HDIM)
    first = lax.broadcasted_iota(jnp.int32, (QHEADS, HDIM), 0) < QHEADS // KVHEADS
    position = lax.broadcasted_iota(jnp.int32, (QHEADS, context), 1)
    all_scores = []
    all_own = []
    for i in range(block):
        q = q_ref[i]
        none = jnp.zeros_like(q)
        wide = jnp.concatenate([jnp.where(first, q, none), jnp.where(first, none, q)], axis=1)
        scores = lax.dot_general(
            wide, k_ref[i], (((1,), (1,)), ((), ())), preferred_element_type=jnp.float32
        )
        all_scores.append(
            jnp.where(position < lengths_ref[step * block + i], scores * scaling, -jnp.inf)
        )
        fresh = nk_ref[i : i + 1, :].astype(jnp.float32)
        all_own.append(jnp.sum(wide.astype(jnp.float32) * fresh, axis=1, keepdims=True) * scaling)
    scores = jnp.concatenate(all_scores, axis=0)
    own = jnp.concatenate(all_own, axis=0)
    highest = jnp.maximum(jnp.max(scores, axis=1, keepdims=True), own)
    powers = jnp.exp(scores - highest)
    own_power = jnp.exp(own - highest)
    inverse = 1.0 / (jnp.sum(powers, axis=1, keepdims=True) + own_power)
    probs = (powers * inverse).astype(jnp.bfloat16)
    own_prob = (own_power * inverse).astype(jnp.bfloat16).astype(jnp.float32)
    for i in range(block):
        span = slice(i * QHEADS, (i + 1) * QHEADS)
        mixed = jnp.dot(probs[span], v_ref[i], preferred_element_type=jnp.float32)
        mixed = mixed + own_prob[span] * nv_ref[i : i + 1, :].astype(jnp.float32)
        at = pl.multiple_of((step * block + i) * QHEADS, QHEADS)
        mixed_ref[pl.ds(at, QHEADS), :] = jnp.where(first, mixed[:, :HDIM], mixed[:, HDIM:])

    @pl.when(step == pl.num_programs(0) - 1)
    def _():
        rows, width = middle_ref.shape
        squares = jnp.zeros((rows, HDIM), jnp.float32)
        for head in range(QHEADS):
            cols = slice(head * HDIM, (head + 1) * HDIM)
            middle = hidden_ref[:, cols].astype(jnp.float32) + mixed_ref[
                pl.ds(head, rows, stride=QHEADS), :
            ]
            middle_ref[:, cols] = middle
            squares = squares + middle * middle
        scale = lax.rsqrt(jnp.sum(squares, axis=1, keepdims=True) / width + 1e-06)
        part = 512
        for at in range(0, width, part):
            cols = slice(at, at + part)
            normed = (middle_ref[:, cols] * scale * gain_ref[:, cols]).astype(jnp.bfloat16)
            outgoing_ref[:, cols] = jnp.dot(
                pick_ref[...], normed, preferred_element_type=jnp.float32
            ).astype(jnp.bfloat16)


def attend_call(lengths, queries, keys, values, new_keys, new_values, hidden_states, gain, pick):
    rows, width = hidden_states.shape
    context, features = keys.shape[1:]
    slots = pick.shape[0]
    block = 8
    whole = lambda shape: pl.BlockSpec(shape, lambda i: (0,) * len(shape))
    return pl.pallas_call(
        attend_kernel,
        grid=(rows // block,),
        out_shape=(
            jax.ShapeDtypeStruct((rows, width), jnp.float32),
            jax.ShapeDtypeStruct((slots, width), jnp.bfloat16),
        ),
        in_specs=[
            pl.BlockSpec(memory_space=pltpu.SMEM),
            pl.BlockSpec((block, QHEADS, HDIM), lambda i: (i, 0, 0)),
            pl.BlockSpec((block, context, features), lambda i: (i, 0, 0)),
            pl.BlockSpec((block, context, features), lambda i: (i, 0, 0)),
            pl.BlockSpec((block, features), lambda i: (i, 0)),
            pl.BlockSpec((block, features), lambda i: (i, 0)),
            whole((rows, width)),
            whole((1, width)),
            whole((slots, rows)),
        ],
        out_specs=(whole((rows, width)), whole((slots, width))),
        scratch_shapes=[pltpu.VMEM((rows * QHEADS, HDIM), jnp.float32)],
        compiler_params=pltpu.CompilerParams(vmem_limit_bytes=40 * MIB),
        cost_estimate=pl.CostEstimate(
            flops=2 * rows * 2 * QHEADS * context * features,
            bytes_accessed=64 * MIB,
            transcendentals=rows * QHEADS * context,
        ),
        name="attend",
    )(
        lengths,
        queries.reshape(rows, QHEADS, HDIM),
        keys,
        values,
        new_keys,
        new_values,
        hidden_states,
        gain.reshape(1, width),
        pick,
    )


def spread_piece(piece):
    half = piece.shape[0] // 2
    prev = lax.ppermute(piece, "z", ZUP)
    succ = lax.ppermute(piece, "z", ZDOWN)
    low_far = lax.ppermute(prev[:half], "z", ZUP)
    high_far = lax.ppermute(succ[half:], "z", ZDOWN)
    return [piece, prev, succ], [low_far, high_far]


def with_other_core(mine):
    parts = mine + [lax.ppermute(part, "core", SWAP) for part in mine]
    return [part.reshape((-1, 8) + part.shape[1:]) for part in parts]


def share_copies(place_ref, parts, tags, lo, target_of, sem, kind=None):
    core = place_ref[1]
    copies = []
    for index, part in enumerate(parts):
        which, first = tags[index % len(tags)]
        if not first <= lo < first + part.shape[0]:
            continue
        c = core if index < len(tags) else 1 - core
        source = part.at[lo - first] if kind is None else part.at[lo - first, :, kind]
        copies.append(pltpu.make_async_copy(source, target_of(which).at[:, c], sem))
    return copies


def share_columns(place_ref, lo, which):
    z = lax.rem(place_ref[0] + STEPS[which], RING)
    return pl.ds(pl.multiple_of(lo * 2048 + z * 512, 512), 512)


def near_kernel(place_ref, rows_any, *refs):
    gate_parts, up_parts = refs[:NEAR_PARTS], refs[NEAR_PARTS : 2 * NEAR_PARTS]
    gate_out, up_out, rows_ref, gate_ref, up_ref, sem = refs[2 * NEAR_PARTS :]
    width = gate_out.shape[1]
    depth = rows_ref.shape[2]
    step = 256
    copies = []
    for lo in range(2):
        group = []
        for which in range(3):
            source = rows_any.at[:, share_columns(place_ref, lo, which)]
            target = rows_ref.at[lo, :, which * 512 : (which + 1) * 512]
            group.append(pltpu.make_async_copy(source, target, sem.at[lo]))
        gate_of = lambda which, lo=lo: gate_ref.at[lo, which]
        up_of = lambda which, lo=lo: up_ref.at[lo, which]
        group += share_copies(place_ref, gate_parts, NEAR_TAGS, lo, gate_of, sem.at[lo])
        group += share_copies(place_ref, up_parts, NEAR_TAGS, lo, up_of, sem.at[lo], 0)
        for copy in group:
            copy.start()
        copies.append(group)
    for lo in range(2):
        for copy in copies[lo]:
            copy.wait()

        @pl.loop(0, width // step)
        def _(i):
            cols = pl.ds(pl.multiple_of(i * step, step), step)
            gate = gate_ref[lo, :, :, :, :, cols].reshape(depth, step)
            up = up_ref[lo, :, :, :, :, cols].reshape(depth, step)
            g = jnp.dot(rows_ref[lo], gate, preferred_element_type=jnp.float32)
            u = jnp.dot(rows_ref[lo], up, preferred_element_type=jnp.float32)
            if lo == 0:
                gate_out[:, cols] = g
                up_out[:, cols] = u
            else:
                gate_out[:, cols] += g
                up_out[:, cols] += u


def near_call(place, rows, gate_parts, up_parts):
    count, depth = rows.shape
    width = gate_parts[0].shape[-1]
    any_place = pl.BlockSpec(memory_space=pl.ANY)
    vmem = pl.BlockSpec(memory_space=pltpu.VMEM)
    weight = pltpu.VMEM((2, 3, 8, 2, 32, width), jnp.bfloat16)
    total = jax.ShapeDtypeStruct((count, width), jnp.float32)
    return pl.pallas_call(
        near_kernel,
        out_shape=(total, total),
        in_specs=[pl.BlockSpec(memory_space=pltpu.SMEM)] + [any_place] * (1 + 2 * NEAR_PARTS),
        out_specs=(vmem, vmem),
        scratch_shapes=[
            pltpu.VMEM((2, count, 3 * 512), jnp.bfloat16),
            weight,
            weight,
            pltpu.SemaphoreType.DMA((2,)),
        ],
        compiler_params=pltpu.CompilerParams(vmem_limit_bytes=52 * MIB),
        cost_estimate=pl.CostEstimate(
            flops=3 * count * depth * width,
            bytes_accessed=3 * depth * width + 2 * count * depth,
            transcendentals=0,
        ),
        name="near",
    )(place, rows, *gate_parts, *up_parts)


def rest_kernel(place_ref, gate_sum, up_sum, rows_any, *refs):
    gate_parts, up_parts = refs[:FAR_PARTS], refs[FAR_PARTS : 2 * FAR_PARTS]
    near_parts = refs[2 * FAR_PARTS : 2 * FAR_PARTS + NEAR_PARTS]
    out_any, rows_ref, gate_ref, up_ref, down_ref, hidden_ref, out_ref, sem, out_sem = refs[
        2 * FAR_PARTS + NEAR_PARTS :
    ]
    width = gate_sum.shape[1]
    step = 256
    copies = []
    for lo in range(2):
        source = rows_any.at[:, share_columns(place_ref, lo, 3)]
        target = rows_ref.at[:, lo * 512 : (lo + 1) * 512]
        copies.append(pltpu.make_async_copy(source, target, sem.at[0]))
        gate_of = lambda which, lo=lo: gate_ref.at[lo]
        up_of = lambda which, lo=lo: up_ref.at[lo]
        copies += share_copies(place_ref, gate_parts, FAR_TAGS, lo, gate_of, sem.at[0])
        copies += share_copies(place_ref, up_parts, FAR_TAGS, lo, up_of, sem.at[0], 0)
    down_copies = []
    for lo in range(2):
        down_of = lambda which, lo=lo: down_ref.at[lo, which]
        group = share_copies(place_ref, near_parts, NEAR_TAGS, lo, down_of, sem.at[1 + lo], 1)
        group += share_copies(place_ref, up_parts, FAR_TAGS, lo, down_of, sem.at[1 + lo], 1)
        down_copies.append(group)
    for copy in copies + down_copies[0] + down_copies[1]:
        copy.start()
    for copy in copies:
        copy.wait()

    @pl.loop(0, width // step)
    def _(i):
        cols = pl.ds(pl.multiple_of(i * step, step), step)
        rows = rows_ref[...]
        gate = gate_ref[:, :, :, :, cols].reshape(1024, step)
        up = up_ref[:, :, :, :, cols].reshape(1024, step)
        g = gate_sum[:, cols] + jnp.dot(rows, gate, preferred_element_type=jnp.float32)
        u = up_sum[:, cols] + jnp.dot(rows, up, preferred_element_type=jnp.float32)
        hidden_ref[:, cols] = (g / (1.0 + jnp.exp(-g)) * u).astype(hidden_ref.dtype)

    outs = []
    for lo in range(2):
        for copy in down_copies[lo]:
            copy.wait()
        for which in range(RING):
            chunk = lo * RING + which
            weight = down_ref[lo, which].reshape(512, width)
            out_ref[chunk] = lax.dot_general(
                hidden_ref[...],
                weight,
                (((1,), (1,)), ((), ())),
                preferred_element_type=jnp.float32,
            ).astype(out_ref.dtype)
            target = out_any.at[:, share_columns(place_ref, lo, which)]
            out = pltpu.make_async_copy(out_ref.at[chunk], target, out_sem.at[chunk])
            out.start()
            outs.append(out)
    for out in outs:
        out.wait()


def rest_call(place, sums, rows, gate_parts, up_parts, near_parts):
    count, depth = rows.shape
    width = gate_parts[0].shape[-1]
    any_place = pl.BlockSpec(memory_space=pl.ANY)
    vmem = pl.BlockSpec(memory_space=pltpu.VMEM)
    weight = pltpu.VMEM((2, 8, 2, 32, width), jnp.bfloat16)
    return pl.pallas_call(
        rest_kernel,
        out_shape=jax.ShapeDtypeStruct((count, depth), jnp.bfloat16),
        in_specs=[pl.BlockSpec(memory_space=pltpu.SMEM), vmem, vmem]
        + [any_place] * (1 + 2 * FAR_PARTS + NEAR_PARTS),
        out_specs=any_place,
        scratch_shapes=[
            pltpu.VMEM((count, 1024), jnp.bfloat16),
            weight,
            weight,
            pltpu.VMEM((2, RING, 8, 2, 32, width), jnp.bfloat16),
            pltpu.VMEM((count, width), jnp.bfloat16),
            pltpu.VMEM((2 * RING, count, 512), jnp.bfloat16),
            pltpu.SemaphoreType.DMA((3,)),
            pltpu.SemaphoreType.DMA((2 * RING,)),
        ],
        compiler_params=pltpu.CompilerParams(vmem_limit_bytes=52 * MIB),
        cost_estimate=pl.CostEstimate(
            flops=3 * count * depth * width,
            bytes_accessed=3 * depth * width + 2 * count * depth,
            transcendentals=count * width,
        ),
        name="rest",
    )(place, *sums, rows, *gate_parts, *up_parts, *near_parts)


def combine_kernel(weighs_ref, picked_ref, middle_ref, back_ref, layer_ref, parcel_ref, rows_ref):
    step = pl.program_id(0)
    back = back_ref[...]
    rows = layer_ref.shape[0]
    routed = jnp.dot(weighs_ref[...], back, preferred_element_type=jnp.float32)
    routed = routed[:rows] + routed[rows:]
    layer = (middle_ref[...] + routed).astype(jnp.bfloat16)
    layer_ref[...] = layer
    lines = picked_ref.shape[0]
    taken = jnp.dot(picked_ref[...], layer, preferred_element_type=jnp.float32)
    per_step = layer.shape[1] // LINE
    for part in range(per_step):
        rows_ref[pl.ds(step * per_step + part, lines, stride=LINES), :] = taken[
            :, part * LINE : (part + 1) * LINE
        ]

    @pl.when(step == pl.num_programs(0) - 1)
    def _():
        parcel_ref[...] = rows_ref[...].reshape(parcel_ref.shape).astype(parcel_ref.dtype)


def combine_call(weighs, picked, middle, back):
    rows, width = middle.shape
    slots = back.shape[0]
    learners = picked.shape[0]
    step = 1024
    whole = lambda shape: pl.BlockSpec(shape, lambda i: (0,) * len(shape))
    column = lambda count: pl.BlockSpec((count, step), lambda i: (0, i))
    return pl.pallas_call(
        combine_kernel,
        grid=(width // step,),
        out_shape=(
            jax.ShapeDtypeStruct((rows, width), jnp.bfloat16),
            jax.ShapeDtypeStruct((learners, LINES, LINE), jnp.bfloat16),
        ),
        in_specs=[
            whole((2 * rows, slots)),
            whole((learners, rows)),
            column(rows),
            column(slots),
        ],
        out_specs=(column(rows), whole((learners, LINES, LINE))),
        scratch_shapes=[pltpu.VMEM((learners * LINES, LINE), jnp.float32)],
        compiler_params=pltpu.CompilerParams(vmem_limit_bytes=16 * MIB),
        name="combine",
    )(weighs, picked, middle, back)


def unpack_kernel(lines_ref, out_ref, rows_ref):
    count = lines_ref.shape[0]
    rows_ref[...] = lines_ref[...].reshape(rows_ref.shape).astype(jnp.float32)
    for part in range(LINES):
        out_ref[:, part * LINE : (part + 1) * LINE] = rows_ref[
            pl.ds(part, count, stride=LINES), :
        ].astype(out_ref.dtype)


def unpack_call(lines):
    count = lines.shape[0]
    block = count // 4
    return pl.pallas_call(
        unpack_kernel,
        grid=(4,),
        out_shape=jax.ShapeDtypeStruct((count, LINES * LINE), jnp.bfloat16),
        in_specs=[pl.BlockSpec((block, LINES, LINE), lambda i: (i, 0, 0))],
        out_specs=pl.BlockSpec((block, LINES * LINE), lambda i: (i, 0)),
        scratch_shapes=[pltpu.VMEM((block * LINES, LINE), jnp.float32)],
        compiler_params=pltpu.CompilerParams(vmem_limit_bytes=16 * MIB),
        name="unpack",
    )(lines)


def shards(
    hidden_states,
    queries,
    key_cache,
    value_cache,
    new_keys,
    new_values,
    cache_lengths,
    norm_gain,
    expert_ids,
    route_weights,
    finished,
    learner_ids,
    gate_weight,
    up_weight,
    down_weight,
):
    experts = 16
    learners = 128
    row_count, model_width = hidden_states.shape
    capacity = row_count // 2
    slots = experts * capacity
    place = jnp.stack([lax.axis_index("z"), lax.axis_index("core")]).astype(jnp.int32)

    to_chip = lambda part: lax.all_to_all(part, PLANE, split_axis=0, concat_axis=0, tiled=True)
    gate = to_chip(gate_weight)
    pair = jnp.stack([up_weight, jnp.swapaxes(down_weight, 1, 2)], axis=1)

    expert_range = jnp.arange(experts, dtype=jnp.int32)
    hit_table = expert_ids[:, :, None] == expert_range[None, None, :]
    matched = jnp.any(hit_table, axis=1)
    slot_gate = jnp.sum(jnp.where(hit_table, route_weights[:, :, None], 0.0), axis=1)
    row_range = jnp.arange(row_count, dtype=jnp.int32)
    earlier = row_range[None, :] < row_range[:, None]
    slot_rank = jnp.sum(
        jnp.where(earlier[:, :, None] & matched[None, :, :], 1, 0).astype(jnp.int32), axis=1
    )
    slot_range = jnp.arange(capacity, dtype=jnp.int32)
    chosen = matched[:, :, None] & (slot_rank[:, :, None] == slot_range[None, None, :])
    weigh = jnp.where(chosen, slot_gate[:, :, None], 0.0).reshape(row_count, slots)
    weigh_high = weigh.astype(jnp.bfloat16)
    weigh_low = (weigh - weigh_high.astype(jnp.float32)).astype(jnp.bfloat16)
    weighs = jnp.concatenate([weigh_high, weigh_low], axis=0)
    turned = matched.T[:, None, :] & (slot_rank.T[:, None, :] == slot_range[None, :, None])
    pick = turned.reshape(slots, row_count).astype(jnp.bfloat16)

    finished_rows = finished > 0
    same_target = (learner_ids[:, None] == learner_ids[None, :]) & finished_rows[None, :] & earlier
    learner_rank = jnp.sum(same_target.astype(jnp.int32), axis=1)
    slot_of_row = learner_ids + learner_rank
    slot_span = jnp.arange(learners, dtype=jnp.int32)
    picked = finished_rows[None, :] & (slot_of_row[None, :] == slot_span[:, None])
    picked = picked.astype(jnp.bfloat16)

    pair, queries, gate, weighs, pick, picked, place = lax.optimization_barrier(
        (pair, queries, gate, weighs, pick, picked, place)
    )
    pair = to_chip(pair)
    gate_near, gate_far = spread_piece(gate)
    middle, outgoing = attend_call(
        cache_lengths,
        queries,
        key_cache,
        value_cache,
        new_keys,
        new_values,
        hidden_states,
        norm_gain,
        pick,
    )
    pair, outgoing, _, _ = lax.optimization_barrier((pair, outgoing, gate_near[1], gate_near[2]))
    pair_near, pair_far = spread_piece(pair)
    received = lax.all_to_all(
        outgoing.reshape(experts, capacity, model_width),
        PLANE,
        split_axis=0,
        concat_axis=0,
        tiled=True,
    ).reshape(slots, model_width)

    pair_near = with_other_core(pair_near)
    sums = near_call(place, received, with_other_core(gate_near), pair_near)
    gate_far = with_other_core(gate_far)
    low_far, high_far, *sums = lax.optimization_barrier((*pair_far, *sums))
    pair_far = with_other_core([low_far, high_far])
    expert_out = rest_call(place, sums, received, gate_far, pair_far, pair_near)
    returned = lax.all_to_all(
        expert_out.reshape(experts, capacity, model_width),
        PLANE,
        split_axis=0,
        concat_axis=0,
        tiled=True,
    ).reshape(slots, model_width)

    layer_out, parcel = combine_call(weighs, picked, middle, returned)
    arrived = lax.all_to_all(parcel, AXES, split_axis=0, concat_axis=0, tiled=True)
    return (layer_out, unpack_call(arrived))


def solution(mesh):
    fine = Mesh(mesh.devices.reshape(2, 4, 4, 2, 2), AXES)
    rows = P(AXES)
    placed = (
        P(AXES, None),
        P(AXES, None),
        P(AXES, None, None),
        P(AXES, None, None),
        P(AXES, None),
        P(AXES, None),
        P(AXES),
        P(),
        P(AXES, None),
        P(AXES, None),
        P(AXES),
        P(AXES),
        P(None, AXES, None),
        P(None, AXES, None),
        P(None, None, AXES),
    )
    return jax.shard_map(
        shards,
        mesh=fine,
        in_specs=placed,
        out_specs=(P(AXES, None), P(AXES, None)),
        check_vma=False,
    )
```

```python
import math

import jax
import jax.numpy as jnp
from jax import lax
from jax.experimental import pallas as pl
from jax.experimental.pallas import tpu as pltpu
from jax.sharding import Mesh
from jax.sharding import PartitionSpec as P

HDIM = 128
QHEADS = 32
KVHEADS = 2

AXES = ("ylo", "z", "x", "yhi", "core")
PLANE = ("ylo", "x", "yhi")
RING = 4
ZUP = [(i, (i + 1) % RING) for i in range(RING)]
ZDOWN = [(i, (i - 1) % RING) for i in range(RING)]
SWAP = [(0, 1), (1, 0)]
STEPS = (0, RING - 1, 1, 2)
NEAR_TAGS = ((0, 0), (1, 0), (2, 0))
FAR_TAGS = ((3, 0), (3, 1))
NEAR_PARTS = 2 * len(NEAR_TAGS)
FAR_PARTS = 2 * len(FAR_TAGS)
LINE = 128
LINES = 32
MIB = 1024 * 1024


def attend_kernel(
    lengths_ref,
    q_ref,
    k_ref,
    v_ref,
    nk_ref,
    nv_ref,
    hidden_ref,
    gain_ref,
    pick_ref,
    middle_ref,
    outgoing_ref,
    mixed_ref,
):
    step = pl.program_id(0)
    block, context, _ = k_ref.shape
    scaling = 1.0 / math.sqrt(HDIM)
    first = lax.broadcasted_iota(jnp.int32, (QHEADS, HDIM), 0) < QHEADS // KVHEADS
    position = lax.broadcasted_iota(jnp.int32, (QHEADS, context), 1)
    all_scores = []
    all_own = []
    for i in range(block):
        q = q_ref[i]
        none = jnp.zeros_like(q)
        wide = jnp.concatenate([jnp.where(first, q, none), jnp.where(first, none, q)], axis=1)
        scores = lax.dot_general(
            wide, k_ref[i], (((1,), (1,)), ((), ())), preferred_element_type=jnp.float32
        )
        all_scores.append(
            jnp.where(position < lengths_ref[step * block + i], scores * scaling, -jnp.inf)
        )
        fresh = nk_ref[i : i + 1, :].astype(jnp.float32)
        all_own.append(jnp.sum(wide.astype(jnp.float32) * fresh, axis=1, keepdims=True) * scaling)
    scores = jnp.concatenate(all_scores, axis=0)
    own = jnp.concatenate(all_own, axis=0)
    highest = jnp.maximum(jnp.max(scores, axis=1, keepdims=True), own)
    powers = jnp.exp(scores - highest)
    own_power = jnp.exp(own - highest)
    inverse = 1.0 / (jnp.sum(powers, axis=1, keepdims=True) + own_power)
    probs = (powers * inverse).astype(jnp.bfloat16)
    own_prob = (own_power * inverse).astype(jnp.bfloat16).astype(jnp.float32)
    for i in range(block):
        span = slice(i * QHEADS, (i + 1) * QHEADS)
        mixed = jnp.dot(probs[span], v_ref[i], preferred_element_type=jnp.float32)
        mixed = mixed + own_prob[span] * nv_ref[i : i + 1, :].astype(jnp.float32)
        at = pl.multiple_of((step * block + i) * QHEADS, QHEADS)
        mixed_ref[pl.ds(at, QHEADS), :] = jnp.where(first, mixed[:, :HDIM], mixed[:, HDIM:])

    @pl.when(step == pl.num_programs(0) - 1)
    def _():
        rows, width = middle_ref.shape
        squares = jnp.zeros((rows, HDIM), jnp.float32)
        for head in range(QHEADS):
            cols = slice(head * HDIM, (head + 1) * HDIM)
            middle = hidden_ref[:, cols].astype(jnp.float32) + mixed_ref[
                pl.ds(head, rows, stride=QHEADS), :
            ]
            middle_ref[:, cols] = middle
            squares = squares + middle * middle
        scale = lax.rsqrt(jnp.sum(squares, axis=1, keepdims=True) / width + 1e-06)
        part = 512
        for at in range(0, width, part):
            cols = slice(at, at + part)
            normed = (middle_ref[:, cols] * scale * gain_ref[:, cols]).astype(jnp.bfloat16)
            outgoing_ref[:, cols] = jnp.dot(
                pick_ref[...], normed, preferred_element_type=jnp.float32
            ).astype(jnp.bfloat16)


def attend_call(lengths, queries, keys, values, new_keys, new_values, hidden_states, gain, pick):
    rows, width = hidden_states.shape
    context, features = keys.shape[1:]
    slots = pick.shape[0]
    block = 8
    whole = lambda shape: pl.BlockSpec(shape, lambda i: (0,) * len(shape))
    return pl.pallas_call(
        attend_kernel,
        grid=(rows // block,),
        out_shape=(
            jax.ShapeDtypeStruct((rows, width), jnp.float32),
            jax.ShapeDtypeStruct((slots, width), jnp.bfloat16),
        ),
        in_specs=[
            pl.BlockSpec(memory_space=pltpu.SMEM),
            pl.BlockSpec((block, QHEADS, HDIM), lambda i: (i, 0, 0)),
            pl.BlockSpec((block, context, features), lambda i: (i, 0, 0)),
            pl.BlockSpec((block, context, features), lambda i: (i, 0, 0)),
            pl.BlockSpec((block, features), lambda i: (i, 0)),
            pl.BlockSpec((block, features), lambda i: (i, 0)),
            whole((rows, width)),
            whole((1, width)),
            whole((slots, rows)),
        ],
        out_specs=(whole((rows, width)), whole((slots, width))),
        scratch_shapes=[pltpu.VMEM((rows * QHEADS, HDIM), jnp.float32)],
        compiler_params=pltpu.CompilerParams(vmem_limit_bytes=40 * MIB),
        cost_estimate=pl.CostEstimate(
            flops=2 * rows * 2 * QHEADS * context * features,
            bytes_accessed=64 * MIB,
            transcendentals=rows * QHEADS * context,
        ),
        name="attend",
    )(
        lengths,
        queries.reshape(rows, QHEADS, HDIM),
        keys,
        values,
        new_keys,
        new_values,
        hidden_states,
        gain.reshape(1, width),
        pick,
    )


def spread_piece(piece):
    half = piece.shape[0] // 2
    prev = lax.ppermute(piece, "z", ZUP)
    succ = lax.ppermute(piece, "z", ZDOWN)
    low_far = lax.ppermute(prev[:half], "z", ZUP)
    high_far = lax.ppermute(succ[half:], "z", ZDOWN)
    return [piece, prev, succ], [low_far, high_far]


def with_other_core(mine):
    parts = mine + [lax.ppermute(part, "core", SWAP) for part in mine]
    return [part.reshape((-1, 8) + part.shape[1:]) for part in parts]


def share_copies(place_ref, parts, tags, lo, target_of, sem, kind=None):
    core = place_ref[1]
    copies = []
    for index, part in enumerate(parts):
        which, first = tags[index % len(tags)]
        if not first <= lo < first + part.shape[0]:
            continue
        c = core if index < len(tags) else 1 - core
        source = part.at[lo - first] if kind is None else part.at[lo - first, :, kind]
        copies.append(pltpu.make_async_copy(source, target_of(which).at[:, c], sem))
    return copies


def share_columns(place_ref, lo, which):
    z = lax.rem(place_ref[0] + STEPS[which], RING)
    return pl.ds(pl.multiple_of(lo * 2048 + z * 512, 512), 512)


def near_kernel(place_ref, rows_any, *refs):
    gate_parts, up_parts = refs[:NEAR_PARTS], refs[NEAR_PARTS : 2 * NEAR_PARTS]
    gate_out, up_out, rows_ref, gate_ref, up_ref, sem = refs[2 * NEAR_PARTS :]
    width = gate_out.shape[1]
    depth = rows_ref.shape[2]
    step = 256
    copies = []
    for lo in range(2):
        group = []
        for which in range(3):
            source = rows_any.at[:, share_columns(place_ref, lo, which)]
            target = rows_ref.at[lo, :, which * 512 : (which + 1) * 512]
            group.append(pltpu.make_async_copy(source, target, sem.at[lo]))
        gate_of = lambda which, lo=lo: gate_ref.at[lo, which]
        up_of = lambda which, lo=lo: up_ref.at[lo, which]
        group += share_copies(place_ref, gate_parts, NEAR_TAGS, lo, gate_of, sem.at[lo])
        group += share_copies(place_ref, up_parts, NEAR_TAGS, lo, up_of, sem.at[lo], 0)
        for copy in group:
            copy.start()
        copies.append(group)
    for lo in range(2):
        for copy in copies[lo]:
            copy.wait()

        @pl.loop(0, width // step)
        def _(i):
            cols = pl.ds(pl.multiple_of(i * step, step), step)
            gate = gate_ref[lo, :, :, :, :, cols].reshape(depth, step)
            up = up_ref[lo, :, :, :, :, cols].reshape(depth, step)
            g = jnp.dot(rows_ref[lo], gate, preferred_element_type=jnp.float32)
            u = jnp.dot(rows_ref[lo], up, preferred_element_type=jnp.float32)
            if lo == 0:
                gate_out[:, cols] = g
                up_out[:, cols] = u
            else:
                gate_out[:, cols] += g
                up_out[:, cols] += u


def near_call(place, rows, gate_parts, up_parts):
    count, depth = rows.shape
    width = gate_parts[0].shape[-1]
    any_place = pl.BlockSpec(memory_space=pl.ANY)
    vmem = pl.BlockSpec(memory_space=pltpu.VMEM)
    weight = pltpu.VMEM((2, 3, 8, 2, 32, width), jnp.bfloat16)
    total = jax.ShapeDtypeStruct((count, width), jnp.float32)
    return pl.pallas_call(
        near_kernel,
        out_shape=(total, total),
        in_specs=[pl.BlockSpec(memory_space=pltpu.SMEM)] + [any_place] * (1 + 2 * NEAR_PARTS),
        out_specs=(vmem, vmem),
        scratch_shapes=[
            pltpu.VMEM((2, count, 3 * 512), jnp.bfloat16),
            weight,
            weight,
            pltpu.SemaphoreType.DMA((2,)),
        ],
        compiler_params=pltpu.CompilerParams(vmem_limit_bytes=52 * MIB),
        cost_estimate=pl.CostEstimate(
            flops=3 * count * depth * width,
            bytes_accessed=3 * depth * width + 2 * count * depth,
            transcendentals=0,
        ),
        name="near",
    )(place, rows, *gate_parts, *up_parts)


def rest_kernel(place_ref, gate_sum, up_sum, rows_any, *refs):
    gate_parts, up_parts = refs[:FAR_PARTS], refs[FAR_PARTS : 2 * FAR_PARTS]
    near_parts = refs[2 * FAR_PARTS : 2 * FAR_PARTS + NEAR_PARTS]
    out_any, rows_ref, gate_ref, up_ref, down_ref, hidden_ref, out_ref, sem, out_sem = refs[
        2 * FAR_PARTS + NEAR_PARTS :
    ]
    width = gate_sum.shape[1]
    step = 256
    copies = []
    for lo in range(2):
        source = rows_any.at[:, share_columns(place_ref, lo, 3)]
        target = rows_ref.at[:, lo * 512 : (lo + 1) * 512]
        copies.append(pltpu.make_async_copy(source, target, sem.at[0]))
        gate_of = lambda which, lo=lo: gate_ref.at[lo]
        up_of = lambda which, lo=lo: up_ref.at[lo]
        copies += share_copies(place_ref, gate_parts, FAR_TAGS, lo, gate_of, sem.at[0])
        copies += share_copies(place_ref, up_parts, FAR_TAGS, lo, up_of, sem.at[0], 0)
    down_copies = []
    for lo in range(2):
        down_of = lambda which, lo=lo: down_ref.at[lo, which]
        group = share_copies(place_ref, near_parts, NEAR_TAGS, lo, down_of, sem.at[1 + lo], 1)
        group += share_copies(place_ref, up_parts, FAR_TAGS, lo, down_of, sem.at[1 + lo], 1)
        down_copies.append(group)
    for copy in copies + down_copies[0] + down_copies[1]:
        copy.start()
    for copy in copies:
        copy.wait()

    @pl.loop(0, width // step)
    def _(i):
        cols = pl.ds(pl.multiple_of(i * step, step), step)
        rows = rows_ref[...]
        gate = gate_ref[:, :, :, :, cols].reshape(1024, step)
        up = up_ref[:, :, :, :, cols].reshape(1024, step)
        g = gate_sum[:, cols] + jnp.dot(rows, gate, preferred_element_type=jnp.float32)
        u = up_sum[:, cols] + jnp.dot(rows, up, preferred_element_type=jnp.float32)
        hidden_ref[:, cols] = (g / (1.0 + jnp.exp(-g)) * u).astype(hidden_ref.dtype)

    outs = []
    for lo in range(2):
        for copy in down_copies[lo]:
            copy.wait()
        for which in range(RING):
            chunk = lo * RING + which
            weight = down_ref[lo, which].reshape(512, width)
            out_ref[chunk] = lax.dot_general(
                hidden_ref[...],
                weight,
                (((1,), (1,)), ((), ())),
                preferred_element_type=jnp.float32,
            ).astype(out_ref.dtype)
            target = out_any.at[:, share_columns(place_ref, lo, which)]
            out = pltpu.make_async_copy(out_ref.at[chunk], target, out_sem.at[chunk])
            out.start()
            outs.append(out)
    for out in outs:
        out.wait()


def rest_call(place, sums, rows, gate_parts, up_parts, near_parts):
    count, depth = rows.shape
    width = gate_parts[0].shape[-1]
    any_place = pl.BlockSpec(memory_space=pl.ANY)
    vmem = pl.BlockSpec(memory_space=pltpu.VMEM)
    weight = pltpu.VMEM((2, 8, 2, 32, width), jnp.bfloat16)
    return pl.pallas_call(
        rest_kernel,
        out_shape=jax.ShapeDtypeStruct((count, depth), jnp.bfloat16),
        in_specs=[pl.BlockSpec(memory_space=pltpu.SMEM), vmem, vmem]
        + [any_place] * (1 + 2 * FAR_PARTS + NEAR_PARTS),
        out_specs=any_place,
        scratch_shapes=[
            pltpu.VMEM((count, 1024), jnp.bfloat16),
            weight,
            weight,
            pltpu.VMEM((2, RING, 8, 2, 32, width), jnp.bfloat16),
            pltpu.VMEM((count, width), jnp.bfloat16),
            pltpu.VMEM((2 * RING, count, 512), jnp.bfloat16),
            pltpu.SemaphoreType.DMA((3,)),
            pltpu.SemaphoreType.DMA((2 * RING,)),
        ],
        compiler_params=pltpu.CompilerParams(vmem_limit_bytes=52 * MIB),
        cost_estimate=pl.CostEstimate(
            flops=3 * count * depth * width,
            bytes_accessed=3 * depth * width + 2 * count * depth,
            transcendentals=count * width,
        ),
        name="rest",
    )(place, *sums, rows, *gate_parts, *up_parts, *near_parts)


def combine_kernel(weighs_ref, picked_ref, middle_ref, back_ref, layer_ref, parcel_ref, rows_ref):
    step = pl.program_id(0)
    back = back_ref[...]
    rows = layer_ref.shape[0]
    routed = jnp.dot(weighs_ref[...], back, preferred_element_type=jnp.float32)
    routed = routed[:rows] + routed[rows:]
    layer = (middle_ref[...] + routed).astype(jnp.bfloat16)
    layer_ref[...] = layer
    lines = picked_ref.shape[0]
    taken = jnp.dot(picked_ref[...], layer, preferred_element_type=jnp.float32)
    per_step = layer.shape[1] // LINE
    for part in range(per_step):
        rows_ref[pl.ds(step * per_step + part, lines, stride=LINES), :] = taken[
            :, part * LINE : (part + 1) * LINE
        ]

    @pl.when(step == pl.num_programs(0) - 1)
    def _():
        parcel_ref[...] = rows_ref[...].reshape(parcel_ref.shape).astype(parcel_ref.dtype)


def combine_call(weighs, picked, middle, back):
    rows, width = middle.shape
    slots = back.shape[0]
    learners = picked.shape[0]
    step = 2048
    whole = lambda shape: pl.BlockSpec(shape, lambda i: (0,) * len(shape))
    column = lambda count: pl.BlockSpec((count, step), lambda i: (0, i))
    return pl.pallas_call(
        combine_kernel,
        grid=(width // step,),
        out_shape=(
            jax.ShapeDtypeStruct((rows, width), jnp.bfloat16),
            jax.ShapeDtypeStruct((learners, LINES, LINE), jnp.bfloat16),
        ),
        in_specs=[
            whole((2 * rows, slots)),
            whole((learners, rows)),
            column(rows),
            column(slots),
        ],
        out_specs=(column(rows), whole((learners, LINES, LINE))),
        scratch_shapes=[pltpu.VMEM((learners * LINES, LINE), jnp.float32)],
        compiler_params=pltpu.CompilerParams(vmem_limit_bytes=16 * MIB),
        name="combine",
    )(weighs, picked, middle, back)


def unpack_kernel(lines_ref, out_ref, rows_ref):
    count = lines_ref.shape[0]
    rows_ref[...] = lines_ref[...].reshape(rows_ref.shape).astype(jnp.float32)
    for part in range(LINES):
        out_ref[:, part * LINE : (part + 1) * LINE] = rows_ref[
            pl.ds(part, count, stride=LINES), :
        ].astype(out_ref.dtype)


def unpack_call(lines):
    count = lines.shape[0]
    block = count // 4
    return pl.pallas_call(
        unpack_kernel,
        grid=(4,),
        out_shape=jax.ShapeDtypeStruct((count, LINES * LINE), jnp.bfloat16),
        in_specs=[pl.BlockSpec((block, LINES, LINE), lambda i: (i, 0, 0))],
        out_specs=pl.BlockSpec((block, LINES * LINE), lambda i: (i, 0)),
        scratch_shapes=[pltpu.VMEM((block * LINES, LINE), jnp.float32)],
        compiler_params=pltpu.CompilerParams(vmem_limit_bytes=16 * MIB),
        name="unpack",
    )(lines)


def shards(
    hidden_states,
    queries,
    key_cache,
    value_cache,
    new_keys,
    new_values,
    cache_lengths,
    norm_gain,
    expert_ids,
    route_weights,
    finished,
    learner_ids,
    gate_weight,
    up_weight,
    down_weight,
):
    experts = 16
    learners = 128
    row_count, model_width = hidden_states.shape
    capacity = row_count // 2
    slots = experts * capacity
    place = jnp.stack([lax.axis_index("z"), lax.axis_index("core")]).astype(jnp.int32)

    to_chip = lambda part: lax.all_to_all(part, PLANE, split_axis=0, concat_axis=0, tiled=True)
    gate = to_chip(gate_weight)
    pair = jnp.stack([up_weight, jnp.swapaxes(down_weight, 1, 2)], axis=1)
    pair, queries, gate = lax.optimization_barrier((pair, queries, gate))
    pair = to_chip(pair)
    gate_near, gate_far = spread_piece(gate)

    expert_range = jnp.arange(experts, dtype=jnp.int32)
    hit_table = expert_ids[:, :, None] == expert_range[None, None, :]
    matched = jnp.any(hit_table, axis=1)
    slot_gate = jnp.sum(jnp.where(hit_table, route_weights[:, :, None], 0.0), axis=1)
    row_range = jnp.arange(row_count, dtype=jnp.int32)
    earlier = row_range[None, :] < row_range[:, None]
    slot_rank = jnp.sum(
        jnp.where(earlier[:, :, None] & matched[None, :, :], 1, 0).astype(jnp.int32), axis=1
    )
    slot_range = jnp.arange(capacity, dtype=jnp.int32)
    chosen = matched[:, :, None] & (slot_rank[:, :, None] == slot_range[None, None, :])
    weigh = jnp.where(chosen, slot_gate[:, :, None], 0.0).reshape(row_count, slots)
    weigh_high = weigh.astype(jnp.bfloat16)
    weigh_low = (weigh - weigh_high.astype(jnp.float32)).astype(jnp.bfloat16)
    weighs = jnp.concatenate([weigh_high, weigh_low], axis=0)
    turned = matched.T[:, None, :] & (slot_rank.T[:, None, :] == slot_range[None, :, None])
    pick = turned.reshape(slots, row_count).astype(jnp.bfloat16)

    finished_rows = finished > 0
    same_target = (learner_ids[:, None] == learner_ids[None, :]) & finished_rows[None, :] & earlier
    learner_rank = jnp.sum(same_target.astype(jnp.int32), axis=1)
    slot_of_row = learner_ids + learner_rank
    slot_span = jnp.arange(learners, dtype=jnp.int32)
    picked = finished_rows[None, :] & (slot_of_row[None, :] == slot_span[:, None])
    picked = picked.astype(jnp.bfloat16)

    queries, weighs, picked, place = lax.optimization_barrier((queries, weighs, picked, place))
    middle, outgoing = attend_call(
        cache_lengths,
        queries,
        key_cache,
        value_cache,
        new_keys,
        new_values,
        hidden_states,
        norm_gain,
        pick,
    )
    pair, outgoing, _, _ = lax.optimization_barrier((pair, outgoing, gate_near[1], gate_near[2]))
    pair_near, pair_far = spread_piece(pair)
    received = lax.all_to_all(
        outgoing.reshape(experts, capacity, model_width),
        PLANE,
        split_axis=0,
        concat_axis=0,
        tiled=True,
    ).reshape(slots, model_width)

    pair_near = with_other_core(pair_near)
    sums = near_call(place, received, with_other_core(gate_near), pair_near)
    gate_far = with_other_core(gate_far)
    low_far, high_far, *sums = lax.optimization_barrier((*pair_far, *sums))
    pair_far = with_other_core([low_far, high_far])
    expert_out = rest_call(place, sums, received, gate_far, pair_far, pair_near)
    returned = lax.all_to_all(
        expert_out.reshape(experts, capacity, model_width),
        PLANE,
        split_axis=0,
        concat_axis=0,
        tiled=True,
    ).reshape(slots, model_width)

    layer_out, parcel = combine_call(weighs, picked, middle, returned)
    arrived = lax.all_to_all(parcel, AXES, split_axis=0, concat_axis=0, tiled=True)
    return (layer_out, unpack_call(arrived))


def solution(mesh):
    fine = Mesh(mesh.devices.reshape(2, 4, 4, 2, 2), AXES)
    rows = P(AXES)
    placed = (
        P(AXES, None),
        P(AXES, None),
        P(AXES, None, None),
        P(AXES, None, None),
        P(AXES, None),
        P(AXES, None),
        P(AXES),
        P(),
        P(AXES, None),
        P(AXES, None),
        P(AXES),
        P(AXES),
        P(None, AXES, None),
        P(None, AXES, None),
        P(None, None, AXES),
    )
    return jax.shard_map(
        shards,
        mesh=fine,
        in_specs=placed,
        out_specs=(P(AXES, None), P(AXES, None)),
        check_vma=False,
    )
```

```python
import math

import jax
import jax.numpy as jnp
from jax import lax
from jax.experimental import pallas as pl
from jax.experimental.pallas import tpu as pltpu
from jax.sharding import Mesh
from jax.sharding import PartitionSpec as P

HDIM = 128
QHEADS = 32
KVHEADS = 2

AXES = ("ylo", "z", "x", "yhi", "core")
PLANE = ("ylo", "x", "yhi")
RING = 4
ZUP = [(i, (i + 1) % RING) for i in range(RING)]
ZDOWN = [(i, (i - 1) % RING) for i in range(RING)]
SWAP = [(0, 1), (1, 0)]
STEPS = (0, RING - 1, 1, 2)
NEAR_TAGS = ((0, 0), (1, 0), (2, 0))
FAR_TAGS = ((3, 0), (3, 1))
NEAR_PARTS = 2 * len(NEAR_TAGS)
FAR_PARTS = 2 * len(FAR_TAGS)
LINE = 128
LINES = 32
MIB = 1024 * 1024


def attend_kernel(
    lengths_ref,
    q_ref,
    k_ref,
    v_ref,
    nk_ref,
    nv_ref,
    hidden_ref,
    gain_ref,
    pick_ref,
    middle_ref,
    outgoing_ref,
    mixed_ref,
):
    step = pl.program_id(0)
    block, context, _ = k_ref.shape
    scaling = 1.0 / math.sqrt(HDIM)
    first = lax.broadcasted_iota(jnp.int32, (QHEADS, HDIM), 0) < QHEADS // KVHEADS
    position = lax.broadcasted_iota(jnp.int32, (QHEADS, context), 1)
    all_scores = []
    all_own = []
    for i in range(block):
        q = q_ref[i]
        none = jnp.zeros_like(q)
        wide = jnp.concatenate([jnp.where(first, q, none), jnp.where(first, none, q)], axis=1)
        scores = lax.dot_general(
            wide, k_ref[i], (((1,), (1,)), ((), ())), preferred_element_type=jnp.float32
        )
        all_scores.append(
            jnp.where(position < lengths_ref[step * block + i], scores * scaling, -jnp.inf)
        )
        fresh = nk_ref[i : i + 1, :].astype(jnp.float32)
        all_own.append(jnp.sum(wide.astype(jnp.float32) * fresh, axis=1, keepdims=True) * scaling)
    scores = jnp.concatenate(all_scores, axis=0)
    own = jnp.concatenate(all_own, axis=0)
    highest = jnp.maximum(jnp.max(scores, axis=1, keepdims=True), own)
    powers = jnp.exp(scores - highest)
    own_power = jnp.exp(own - highest)
    inverse = 1.0 / (jnp.sum(powers, axis=1, keepdims=True) + own_power)
    probs = (powers * inverse).astype(jnp.bfloat16)
    own_prob = (own_power * inverse).astype(jnp.bfloat16).astype(jnp.float32)
    for i in range(block):
        span = slice(i * QHEADS, (i + 1) * QHEADS)
        mixed = jnp.dot(probs[span], v_ref[i], preferred_element_type=jnp.float32)
        mixed = mixed + own_prob[span] * nv_ref[i : i + 1, :].astype(jnp.float32)
        at = pl.multiple_of((step * block + i) * QHEADS, QHEADS)
        mixed_ref[pl.ds(at, QHEADS), :] = jnp.where(first, mixed[:, :HDIM], mixed[:, HDIM:])

    @pl.when(step == pl.num_programs(0) - 1)
    def _():
        rows, width = middle_ref.shape
        squares = jnp.zeros((rows, HDIM), jnp.float32)
        for head in range(QHEADS):
            cols = slice(head * HDIM, (head + 1) * HDIM)
            middle = hidden_ref[:, cols].astype(jnp.float32) + mixed_ref[
                pl.ds(head, rows, stride=QHEADS), :
            ]
            middle_ref[:, cols] = middle
            squares = squares + middle * middle
        scale = lax.rsqrt(jnp.sum(squares, axis=1, keepdims=True) / width + 1e-06)
        part = 512
        for at in range(0, width, part):
            cols = slice(at, at + part)
            normed = (middle_ref[:, cols] * scale * gain_ref[:, cols]).astype(jnp.bfloat16)
            outgoing_ref[:, cols] = jnp.dot(
                pick_ref[...], normed, preferred_element_type=jnp.float32
            ).astype(jnp.bfloat16)


def attend_call(lengths, queries, keys, values, new_keys, new_values, hidden_states, gain, pick):
    rows, width = hidden_states.shape
    context, features = keys.shape[1:]
    slots = pick.shape[0]
    block = 8
    whole = lambda shape: pl.BlockSpec(shape, lambda i: (0,) * len(shape))
    return pl.pallas_call(
        attend_kernel,
        grid=(rows // block,),
        out_shape=(
            jax.ShapeDtypeStruct((rows, width), jnp.float32),
            jax.ShapeDtypeStruct((slots, width), jnp.bfloat16),
        ),
        in_specs=[
            pl.BlockSpec(memory_space=pltpu.SMEM),
            pl.BlockSpec((block, QHEADS, HDIM), lambda i: (i, 0, 0)),
            pl.BlockSpec((block, context, features), lambda i: (i, 0, 0)),
            pl.BlockSpec((block, context, features), lambda i: (i, 0, 0)),
            pl.BlockSpec((block, features), lambda i: (i, 0)),
            pl.BlockSpec((block, features), lambda i: (i, 0)),
            whole((rows, width)),
            whole((1, width)),
            whole((slots, rows)),
        ],
        out_specs=(whole((rows, width)), whole((slots, width))),
        scratch_shapes=[pltpu.VMEM((rows * QHEADS, HDIM), jnp.float32)],
        compiler_params=pltpu.CompilerParams(vmem_limit_bytes=40 * MIB),
        cost_estimate=pl.CostEstimate(
            flops=2 * rows * 2 * QHEADS * context * features,
            bytes_accessed=64 * MIB,
            transcendentals=rows * QHEADS * context,
        ),
        name="attend",
    )(
        lengths,
        queries.reshape(rows, QHEADS, HDIM),
        keys,
        values,
        new_keys,
        new_values,
        hidden_states,
        gain.reshape(1, width),
        pick,
    )


def spread_piece(piece):
    half = piece.shape[0] // 2
    prev = lax.ppermute(piece, "z", ZUP)
    succ = lax.ppermute(piece, "z", ZDOWN)
    low_far = lax.ppermute(prev[:half], "z", ZUP)
    high_far = lax.ppermute(succ[half:], "z", ZDOWN)
    return [piece, prev, succ], [low_far, high_far]


def with_other_core(mine):
    parts = mine + [lax.ppermute(part, "core", SWAP) for part in mine]
    return [part.reshape((-1, 8) + part.shape[1:]) for part in parts]


def share_copies(place_ref, parts, tags, lo, target_of, sem, kind=None):
    core = place_ref[1]
    copies = []
    for index, part in enumerate(parts):
        which, first = tags[index % len(tags)]
        if not first <= lo < first + part.shape[0]:
            continue
        c = core if index < len(tags) else 1 - core
        source = part.at[lo - first] if kind is None else part.at[lo - first, :, kind]
        copies.append(pltpu.make_async_copy(source, target_of(which).at[:, c], sem))
    return copies


def share_columns(place_ref, lo, which):
    z = lax.rem(place_ref[0] + STEPS[which], RING)
    return pl.ds(pl.multiple_of(lo * 2048 + z * 512, 512), 512)


def near_kernel(place_ref, rows_any, *refs):
    gate_parts, up_parts = refs[:NEAR_PARTS], refs[NEAR_PARTS : 2 * NEAR_PARTS]
    gate_out, up_out, rows_ref, gate_ref, up_ref, sem = refs[2 * NEAR_PARTS :]
    width = gate_out.shape[1]
    depth = rows_ref.shape[2]
    step = 256
    copies = []
    for lo in range(2):
        group = []
        for which in range(3):
            source = rows_any.at[:, share_columns(place_ref, lo, which)]
            target = rows_ref.at[lo, :, which * 512 : (which + 1) * 512]
            group.append(pltpu.make_async_copy(source, target, sem.at[lo]))
        gate_of = lambda which, lo=lo: gate_ref.at[lo, which]
        up_of = lambda which, lo=lo: up_ref.at[lo, which]
        group += share_copies(place_ref, gate_parts, NEAR_TAGS, lo, gate_of, sem.at[lo])
        group += share_copies(place_ref, up_parts, NEAR_TAGS, lo, up_of, sem.at[lo], 0)
        for copy in group:
            copy.start()
        copies.append(group)
    for lo in range(2):
        for copy in copies[lo]:
            copy.wait()

        @pl.loop(0, width // step)
        def _(i):
            cols = pl.ds(pl.multiple_of(i * step, step), step)
            gate = gate_ref[lo, :, :, :, :, cols].reshape(depth, step)
            up = up_ref[lo, :, :, :, :, cols].reshape(depth, step)
            g = jnp.dot(rows_ref[lo], gate, preferred_element_type=jnp.float32)
            u = jnp.dot(rows_ref[lo], up, preferred_element_type=jnp.float32)
            if lo == 0:
                gate_out[:, cols] = g
                up_out[:, cols] = u
            else:
                gate_out[:, cols] += g
                up_out[:, cols] += u


def near_call(place, rows, gate_parts, up_parts):
    count, depth = rows.shape
    width = gate_parts[0].shape[-1]
    any_place = pl.BlockSpec(memory_space=pl.ANY)
    vmem = pl.BlockSpec(memory_space=pltpu.VMEM)
    weight = pltpu.VMEM((2, 3, 8, 2, 32, width), jnp.bfloat16)
    total = jax.ShapeDtypeStruct((count, width), jnp.float32)
    return pl.pallas_call(
        near_kernel,
        out_shape=(total, total),
        in_specs=[pl.BlockSpec(memory_space=pltpu.SMEM)] + [any_place] * (1 + 2 * NEAR_PARTS),
        out_specs=(vmem, vmem),
        scratch_shapes=[
            pltpu.VMEM((2, count, 3 * 512), jnp.bfloat16),
            weight,
            weight,
            pltpu.SemaphoreType.DMA((2,)),
        ],
        compiler_params=pltpu.CompilerParams(vmem_limit_bytes=52 * MIB),
        cost_estimate=pl.CostEstimate(
            flops=3 * count * depth * width,
            bytes_accessed=3 * depth * width + 2 * count * depth,
            transcendentals=0,
        ),
        name="near",
    )(place, rows, *gate_parts, *up_parts)


def rest_kernel(place_ref, gate_sum, up_sum, rows_any, *refs):
    gate_parts, up_parts = refs[:FAR_PARTS], refs[FAR_PARTS : 2 * FAR_PARTS]
    near_parts = refs[2 * FAR_PARTS : 2 * FAR_PARTS + NEAR_PARTS]
    out_any, rows_ref, gate_ref, up_ref, down_ref, hidden_ref, out_ref, sem, out_sem = refs[
        2 * FAR_PARTS + NEAR_PARTS :
    ]
    width = gate_sum.shape[1]
    step = 256
    copies = []
    for lo in range(2):
        source = rows_any.at[:, share_columns(place_ref, lo, 3)]
        target = rows_ref.at[:, lo * 512 : (lo + 1) * 512]
        copies.append(pltpu.make_async_copy(source, target, sem.at[0]))
        gate_of = lambda which, lo=lo: gate_ref.at[lo]
        up_of = lambda which, lo=lo: up_ref.at[lo]
        copies += share_copies(place_ref, gate_parts, FAR_TAGS, lo, gate_of, sem.at[0])
        copies += share_copies(place_ref, up_parts, FAR_TAGS, lo, up_of, sem.at[0], 0)
    down_copies = []
    for lo in range(2):
        down_of = lambda which, lo=lo: down_ref.at[lo, which]
        group = share_copies(place_ref, near_parts, NEAR_TAGS, lo, down_of, sem.at[1 + lo], 1)
        group += share_copies(place_ref, up_parts, FAR_TAGS, lo, down_of, sem.at[1 + lo], 1)
        down_copies.append(group)
    for copy in copies + down_copies[0] + down_copies[1]:
        copy.start()
    for copy in copies:
        copy.wait()

    @pl.loop(0, width // step)
    def _(i):
        cols = pl.ds(pl.multiple_of(i * step, step), step)
        rows = rows_ref[...]
        gate = gate_ref[:, :, :, :, cols].reshape(1024, step)
        up = up_ref[:, :, :, :, cols].reshape(1024, step)
        g = gate_sum[:, cols] + jnp.dot(rows, gate, preferred_element_type=jnp.float32)
        u = up_sum[:, cols] + jnp.dot(rows, up, preferred_element_type=jnp.float32)
        hidden_ref[:, cols] = (g / (1.0 + jnp.exp(-g)) * u).astype(hidden_ref.dtype)

    outs = []
    for lo in range(2):
        for copy in down_copies[lo]:
            copy.wait()
        for which in range(RING):
            chunk = lo * RING + which
            weight = down_ref[lo, which].reshape(512, width)
            out_ref[chunk] = lax.dot_general(
                hidden_ref[...],
                weight,
                (((1,), (1,)), ((), ())),
                preferred_element_type=jnp.float32,
            ).astype(out_ref.dtype)
            target = out_any.at[:, share_columns(place_ref, lo, which)]
            out = pltpu.make_async_copy(out_ref.at[chunk], target, out_sem.at[chunk])
            out.start()
            outs.append(out)
    for out in outs:
        out.wait()


def rest_call(place, sums, rows, gate_parts, up_parts, near_parts):
    count, depth = rows.shape
    width = gate_parts[0].shape[-1]
    any_place = pl.BlockSpec(memory_space=pl.ANY)
    vmem = pl.BlockSpec(memory_space=pltpu.VMEM)
    weight = pltpu.VMEM((2, 8, 2, 32, width), jnp.bfloat16)
    return pl.pallas_call(
        rest_kernel,
        out_shape=jax.ShapeDtypeStruct((count, depth), jnp.bfloat16),
        in_specs=[pl.BlockSpec(memory_space=pltpu.SMEM), vmem, vmem]
        + [any_place] * (1 + 2 * FAR_PARTS + NEAR_PARTS),
        out_specs=any_place,
        scratch_shapes=[
            pltpu.VMEM((count, 1024), jnp.bfloat16),
            weight,
            weight,
            pltpu.VMEM((2, RING, 8, 2, 32, width), jnp.bfloat16),
            pltpu.VMEM((count, width), jnp.bfloat16),
            pltpu.VMEM((2 * RING, count, 512), jnp.bfloat16),
            pltpu.SemaphoreType.DMA((3,)),
            pltpu.SemaphoreType.DMA((2 * RING,)),
        ],
        compiler_params=pltpu.CompilerParams(vmem_limit_bytes=52 * MIB),
        cost_estimate=pl.CostEstimate(
            flops=3 * count * depth * width,
            bytes_accessed=3 * depth * width + 2 * count * depth,
            transcendentals=count * width,
        ),
        name="rest",
    )(place, *sums, rows, *gate_parts, *up_parts, *near_parts)


def combine_kernel(weighs_ref, picked_ref, middle_ref, back_ref, layer_ref, parcel_ref, rows_ref):
    step = pl.program_id(0)
    back = back_ref[...]
    rows = layer_ref.shape[0]
    routed = jnp.dot(weighs_ref[...], back, preferred_element_type=jnp.float32)
    routed = routed[:rows] + routed[rows:]
    layer = (middle_ref[...] + routed).astype(jnp.bfloat16)
    layer_ref[...] = layer
    lines = picked_ref.shape[0]
    taken = jnp.dot(picked_ref[...], layer, preferred_element_type=jnp.float32)
    per_step = layer.shape[1] // LINE
    for part in range(per_step):
        rows_ref[pl.ds(step * per_step + part, lines, stride=LINES), :] = taken[
            :, part * LINE : (part + 1) * LINE
        ]

    @pl.when(step == pl.num_programs(0) - 1)
    def _():
        parcel_ref[...] = rows_ref[...].reshape(parcel_ref.shape).astype(parcel_ref.dtype)


def combine_call(weighs, picked, middle, back):
    rows, width = middle.shape
    slots = back.shape[0]
    learners = picked.shape[0]
    step = 2048
    whole = lambda shape: pl.BlockSpec(shape, lambda i: (0,) * len(shape))
    column = lambda count: pl.BlockSpec((count, step), lambda i: (0, i))
    return pl.pallas_call(
        combine_kernel,
        grid=(width // step,),
        out_shape=(
            jax.ShapeDtypeStruct((rows, width), jnp.bfloat16),
            jax.ShapeDtypeStruct((learners, LINES, LINE), jnp.bfloat16),
        ),
        in_specs=[
            whole((2 * rows, slots)),
            whole((learners, rows)),
            column(rows),
            column(slots),
        ],
        out_specs=(column(rows), whole((learners, LINES, LINE))),
        scratch_shapes=[pltpu.VMEM((learners * LINES, LINE), jnp.float32)],
        compiler_params=pltpu.CompilerParams(vmem_limit_bytes=16 * MIB),
        name="combine",
    )(weighs, picked, middle, back)


def unpack_kernel(lines_ref, out_ref, rows_ref):
    count = lines_ref.shape[0]
    rows_ref[...] = lines_ref[...].reshape(rows_ref.shape).astype(jnp.float32)
    for part in range(LINES):
        out_ref[:, part * LINE : (part + 1) * LINE] = rows_ref[
            pl.ds(part, count, stride=LINES), :
        ].astype(out_ref.dtype)


def unpack_call(lines):
    count = lines.shape[0]
    block = count // 4
    return pl.pallas_call(
        unpack_kernel,
        grid=(4,),
        out_shape=jax.ShapeDtypeStruct((count, LINES * LINE), jnp.bfloat16),
        in_specs=[pl.BlockSpec((block, LINES, LINE), lambda i: (i, 0, 0))],
        out_specs=pl.BlockSpec((block, LINES * LINE), lambda i: (i, 0)),
        scratch_shapes=[pltpu.VMEM((block * LINES, LINE), jnp.float32)],
        compiler_params=pltpu.CompilerParams(vmem_limit_bytes=16 * MIB),
        name="unpack",
    )(lines)


def shards(
    hidden_states,
    queries,
    key_cache,
    value_cache,
    new_keys,
    new_values,
    cache_lengths,
    norm_gain,
    expert_ids,
    route_weights,
    finished,
    learner_ids,
    gate_weight,
    up_weight,
    down_weight,
):
    experts = 16
    learners = 128
    row_count, model_width = hidden_states.shape
    capacity = row_count // 2
    slots = experts * capacity
    place = jnp.stack([lax.axis_index("z"), lax.axis_index("core")]).astype(jnp.int32)

    to_chip = lambda part: lax.all_to_all(part, PLANE, split_axis=0, concat_axis=0, tiled=True)
    gate = to_chip(gate_weight)
    pair = jnp.stack([up_weight, jnp.swapaxes(down_weight, 1, 2)], axis=1)

    expert_range = jnp.arange(experts, dtype=jnp.int32)
    hit_table = expert_ids[:, :, None] == expert_range[None, None, :]
    matched = jnp.any(hit_table, axis=1)
    slot_gate = jnp.sum(jnp.where(hit_table, route_weights[:, :, None], 0.0), axis=1)
    row_range = jnp.arange(row_count, dtype=jnp.int32)
    earlier = row_range[None, :] < row_range[:, None]
    slot_rank = jnp.sum(
        jnp.where(earlier[:, :, None] & matched[None, :, :], 1, 0).astype(jnp.int32), axis=1
    )
    slot_range = jnp.arange(capacity, dtype=jnp.int32)
    chosen = matched[:, :, None] & (slot_rank[:, :, None] == slot_range[None, None, :])
    weigh = jnp.where(chosen, slot_gate[:, :, None], 0.0).reshape(row_count, slots)
    weigh_high = weigh.astype(jnp.bfloat16)
    weigh_low = (weigh - weigh_high.astype(jnp.float32)).astype(jnp.bfloat16)
    weighs = jnp.concatenate([weigh_high, weigh_low], axis=0)
    turned = matched.T[:, None, :] & (slot_rank.T[:, None, :] == slot_range[None, :, None])
    pick = turned.reshape(slots, row_count).astype(jnp.bfloat16)

    finished_rows = finished > 0
    same_target = (learner_ids[:, None] == learner_ids[None, :]) & finished_rows[None, :] & earlier
    learner_rank = jnp.sum(same_target.astype(jnp.int32), axis=1)
    slot_of_row = learner_ids + learner_rank
    slot_span = jnp.arange(learners, dtype=jnp.int32)
    picked = finished_rows[None, :] & (slot_of_row[None, :] == slot_span[:, None])
    picked = picked.astype(jnp.bfloat16)

    pair, queries, gate, weighs, pick, picked, place = lax.optimization_barrier(
        (pair, queries, gate, weighs, pick, picked, place)
    )
    pair = to_chip(pair)
    gate_near, gate_far = spread_piece(gate)
    middle, outgoing = attend_call(
        cache_lengths,
        queries,
        key_cache,
        value_cache,
        new_keys,
        new_values,
        hidden_states,
        norm_gain,
        pick,
    )
    pair, outgoing, _, _ = lax.optimization_barrier((pair, outgoing, gate_near[1], gate_near[2]))
    pair_near, pair_far = spread_piece(pair)
    received = lax.all_to_all(
        outgoing.reshape(experts, capacity, model_width),
        PLANE,
        split_axis=0,
        concat_axis=0,
        tiled=True,
    ).reshape(slots, model_width)

    pair_near = with_other_core(pair_near)
    sums = near_call(place, received, with_other_core(gate_near), pair_near)
    gate_far = with_other_core(gate_far)
    low_far, high_far, *sums = lax.optimization_barrier((*pair_far, *sums))
    pair_far = with_other_core([low_far, high_far])
    expert_out = rest_call(place, sums, received, gate_far, pair_far, pair_near)
    returned = lax.all_to_all(
        expert_out.reshape(experts, capacity, model_width),
        PLANE,
        split_axis=0,
        concat_axis=0,
        tiled=True,
    ).reshape(slots, model_width)

    layer_out, parcel = combine_call(weighs, picked, middle, returned)
    arrived = lax.all_to_all(parcel, AXES, split_axis=0, concat_axis=0, tiled=True)
    return (layer_out, unpack_call(arrived))


def solution(mesh):
    fine = Mesh(mesh.devices.reshape(2, 4, 4, 2, 2), AXES)
    rows = P(AXES)
    placed = (
        P(AXES, None),
        P(AXES, None),
        P(AXES, None, None),
        P(AXES, None, None),
        P(AXES, None),
        P(AXES, None),
        P(AXES),
        P(),
        P(AXES, None),
        P(AXES, None),
        P(AXES),
        P(AXES),
        P(None, AXES, None),
        P(None, AXES, None),
        P(None, None, AXES),
    )
    return jax.shard_map(
        shards,
        mesh=fine,
        in_specs=placed,
        out_specs=(P(AXES, None), P(AXES, None)),
        check_vma=False,
    )
```
